256 devices in a mesh: ctx: 64 (over x, z, core), head: 4 (over y).
Axes of the slice: x: 4, y: 4, z: 8, core: 2. Of those that a mesh axis runs over, the one named last changes fastest.
Arguments:
- queries: bfloat16 [2048, 8192], P('ctx', 'head'), may hold values from -8 to 8
- cache_keys: bfloat16 [262144, 1024], P('ctx', 'head'), may hold values from -5 to 5
- cache_values: bfloat16 [262144, 1024], P('ctx', 'head'), may hold values from -6 to 6
- new_keys: bfloat16 [2048, 1024], P('ctx', 'head'), may hold values from -5 to 5
- new_values: bfloat16 [2048, 1024], P('ctx', 'head'), may hold values from -6 to 6
- vertical: int32 [8, 8], P('head'), may hold values from 0 to 4095, as said below
- slash: int32 [8, 4], P('head'), may hold values from 32 to 4096, as said below
Outputs:
- attended: bfloat16 [2048, 8192], P(('ctx', 'head'))
The draws below stay inside these ranges and needn't reach their ends.
Inputs may be any that keep to these rules, and one draw needn't show every extreme that they name: `vertical`: each row names 8 different key blocks and always includes block 0 and block 4095. `slash`: each row holds 4 different offsets and always includes 32 and 4096.
All inputs are finite; a program needn't handle non-finite values.
Results may differ from the reference program's by a relative error of at most 0.008.
Values may be sent and summed in bfloat16 or wider, within the bound.
No kernel may reach another device: no remote copies, remote signals or barrier semaphores. Data moves between devices by JAX's collectives and lax.ppermute only.
A program may use at most 192 MiB of HBM per device.

```python
import math
import jax
import jax.numpy as jnp
from jax import lax

HEADS = 64
KVH = 8
HD = 128
BLOCK = 64
NV = 8
NS = 4
GROUP = 8
QUERIES = 2048
CONTEXT = 262144
QBLOCKS = 32
STORED_TILES = 4096
STORED_EACH_PART = 64


def drawn_rows(key, rows, heads, spread, bound):
    base = spread * jax.random.normal(key, (rows, heads * HD), jnp.float32)
    return jnp.clip(base, -bound, bound)


def draw_queries(key, part):
    key = jax.random.fold_in(key, 1)
    return drawn_rows(key, QUERIES, HEADS, 2.0, 8.0).astype(jnp.bfloat16)


def draw_cache_keys(key, part):
    key = jax.random.fold_in(key, 2)
    return drawn_rows(key, CONTEXT, KVH, 1.0, 5.0).astype(jnp.bfloat16)


def draw_new_keys(key, part):
    key = jax.random.fold_in(key, 3)
    return drawn_rows(key, QUERIES, KVH, 1.0, 5.0).astype(jnp.bfloat16)


def draw_vertical(key, part):
    key = jax.random.fold_in(key, 7)
    noise_key = jax.random.fold_in(key, 1)
    far_key = jax.random.fold_in(key, 2)
    stochastic_jitter = jax.random.randint(noise_key, (KVH, STORED_TILES), 0, 1000)
    tile_sequence = jnp.arange(STORED_TILES, dtype=jnp.int32)
    quarter = STORED_TILES // 4
    far_blocks = jnp.arange(4, dtype=jnp.int32)[None, :] * quarter + jax.random.randint(far_key, (KVH, 4), 0, quarter)
    remote_agreement = jnp.any(tile_sequence[None, None, :] == far_blocks[:, :, None], axis=1)
    remote_uplift = jnp.where(remote_agreement, 50000, 0)
    relevance_uplift = jnp.where(tile_sequence >= STORED_TILES - 4 * STORED_EACH_PART, 600, 0)
    anchored_tiles = jnp.where((tile_sequence == 0) | (tile_sequence == STORED_TILES - 1), 100000, 0)
    tile_relevance = (stochastic_jitter + relevance_uplift[None, :] + anchored_tiles[None, :] + remote_uplift) * STORED_TILES + tile_sequence[None, :]
    _, chosen = lax.top_k(tile_relevance, NV)
    return chosen.astype(jnp.int32)


def draw_slash(key, part):
    key = jax.random.fold_in(key, 9)
    span = STORED_TILES - QBLOCKS + 1
    stochastic_jitter = jax.random.randint(key, (KVH, span), 0, 1000)
    steps = jnp.arange(span, dtype=jnp.int32)
    anchored_tiles = jnp.where((steps == 0) | (steps == span - 1), 100000, 0)
    tile_relevance = (stochastic_jitter + anchored_tiles[None, :]) * span + steps[None, :]
    _, chosen = lax.top_k(tile_relevance, NS)
    return (chosen + QBLOCKS).astype(jnp.int32)


def levels(key, extent, cuts, low, largest):
    def one(dim, shards_of):
        steps = jax.random.uniform(jax.random.fold_in(jax.random.fold_in(key, 6), dim), (shards_of,), jnp.float32, low / len(cuts), largest / len(cuts))
        return jnp.repeat(jnp.exp(steps), extent[dim] // shards_of).reshape((-1,) + (1,) * (len(extent) - dim - 1))

    factor_of = one(*cuts[0])
    for cut in cuts[1:]:
        factor_of = factor_of * one(*cut)
    return factor_of


def normal_values(key, extent, scale, reach, shards=(), kind=jnp.bfloat16):
    entries = scale * jax.random.normal(key, extent, jnp.float32)
    if shards:
        entries = entries * levels(key, extent, shards, -0.22, 0.18)
    return jnp.clip(entries, -reach, reach).astype(kind)


def setup_inputs(seed: int = 0) -> dict:
    arg_keys = jax.random.split(jax.random.key(seed), 8)
    return {
        "queries": draw_queries(jax.random.fold_in(arg_keys[7], 71), 0),
        "cache_keys": draw_cache_keys(jax.random.fold_in(arg_keys[7], 71), 0),
        "cache_values": normal_values(arg_keys[2], (CONTEXT, KVH * HD), 1.0, 6.0, ((0, 64), (1, 4))),
        "new_keys": draw_new_keys(jax.random.fold_in(arg_keys[7], 71), 0),
        "new_values": normal_values(arg_keys[4], (QUERIES, KVH * HD), 1.0, 6.0, ((0, 64), (1, 4))),
        "vertical": draw_vertical(jax.random.fold_in(arg_keys[7], 71), 0),
        "slash": draw_slash(jax.random.fold_in(arg_keys[7], 71), 0),
    }


NEGATIVE = -1e+30

def head_attention(items):
    query_tile, key_tile, value_tile, recent_keys, fresh_values, vert_row, slash_row = items
    softmax_scale = 1.0 / math.sqrt(HD)
    query_broadcast = query_tile.astype(jnp.float32)
    vert_keys = key_tile[vert_row].reshape(NV * BLOCK, HD).astype(jnp.float32)
    vert_values = value_tile[vert_row].reshape(NV * BLOCK, HD)
    slash_blocks = (STORED_TILES + jnp.arange(QBLOCKS, dtype=jnp.int32)[:, None] - slash_row[None, :]).astype(jnp.int32)
    repeated = jnp.any(slash_blocks[:, :, None] == vert_row[None, None, :], axis=-1)
    diagonal_keys = key_tile[slash_blocks].reshape(QBLOCKS, NS * BLOCK, HD).astype(jnp.float32)
    slash_values = value_tile[slash_blocks].reshape(QBLOCKS, NS * BLOCK, HD)
    score_vert = jnp.einsum('bqgd,kd->bqgk', query_broadcast, vert_keys) * softmax_scale
    diagonal_score = jnp.einsum('tucz,tvz->tucv', query_broadcast, diagonal_keys) * softmax_scale
    recent_score = jnp.einsum('tucz,tvz->tucv', query_broadcast, recent_keys.astype(jnp.float32)) * softmax_scale
    keep_vert = jnp.ones(score_vert.shape, dtype=bool)
    keep_slash = jnp.broadcast_to(jnp.repeat(jnp.logical_not(repeated), BLOCK, axis=1)[:, None, None, :], diagonal_score.shape)
    causal = jnp.arange(BLOCK)[None, :] <= jnp.arange(BLOCK)[:, None]
    keep_fresh = jnp.broadcast_to(causal[None, :, None, :], recent_score.shape)
    score_matrix = jnp.concatenate([score_vert, diagonal_score, recent_score], axis=-1)
    allowed_mask = jnp.concatenate([keep_vert, keep_slash, keep_fresh], axis=-1)
    masked = jnp.where(allowed_mask, score_matrix, NEGATIVE)
    peak = lax.optimization_barrier(jnp.max(masked, axis=-1))
    weights = jnp.where(allowed_mask, jnp.exp(masked - peak[..., None]), 0.0)
    total = lax.optimization_barrier(jnp.sum(weights, axis=-1))
    rounded_values = lax.optimization_barrier(weights.astype(jnp.bfloat16))
    value_rows = jnp.concatenate([jnp.broadcast_to(vert_values[None], (QBLOCKS, NV * BLOCK, HD)), slash_values, fresh_values], axis=1)
    summed_result = jnp.einsum('ycex,yxp->ycep', rounded_values.astype(jnp.float32), value_rows.astype(jnp.float32))
    return summed_result / total[..., None]

def reference(queries, cache_keys, cache_values, new_keys, new_values, vertical, slash):
    query_tiles = queries.reshape(QBLOCKS, BLOCK, KVH, GROUP, HD).transpose(2, 0, 1, 3, 4)
    key_tiles = cache_keys.reshape(STORED_TILES, BLOCK, KVH, HD).transpose(2, 0, 1, 3)
    value_tiles = cache_values.reshape(STORED_TILES, BLOCK, KVH, HD).transpose(2, 0, 1, 3)
    recent_keys = new_keys.reshape(QBLOCKS, BLOCK, KVH, HD).transpose(2, 0, 1, 3)
    fresh_values = new_values.reshape(QBLOCKS, BLOCK, KVH, HD).transpose(2, 0, 1, 3)
    result = lax.map(head_attention, (query_tiles, key_tiles, value_tiles, recent_keys, fresh_values, vertical, slash))
    return result.transpose(1, 2, 0, 3, 4).reshape(QUERIES, HEADS * HD).astype(jnp.bfloat16)
```

```python
import math

import jax
import jax.numpy as jnp
from jax import lax
from jax.experimental import pallas as pl
from jax.experimental.pallas import tpu as pltpu
from jax.sharding import Mesh, PartitionSpec as P

HD = 128
BLOCK = 64
NV = 8
NS = 4
GROUP = 8
STORED = 4096
PER_CHIP = 128
LANES = 2
NEGATIVE = -1e30
SLOTS = 4 * LANES * 2 + 2
SLOTS2 = NS * 2 + 2

SMEM = pl.BlockSpec(memory_space=pltpu.SMEM)
HBM = pl.BlockSpec(memory_space=pl.ANY)
VMEM = pl.BlockSpec(memory_space=pltpu.VMEM)


def member(chip):
    return (chip >> 3) * 2 + (chip & 1)


def plane_row(chip):
    return (chip >> 1) & 3


def lane_of(slash, core, j, block, chip):
    rank = jnp.int32(0)
    for i in range(j):
        rank = rank + jnp.where((STORED + block - slash[core, i]) >> 7 == chip, 1, 0)
    return rank


def copy_tiles(sem, count, like):
    def one(_, carry):
        pltpu.make_async_copy(like, like, sem).wait()
        return carry

    lax.fori_loop(0, count, one, 0)


def pack_first(place, slash, vertical, keys, values, out, sem, *, low, vert):
    chip, core = place[0], place[1]
    lanes = LANES if vert else 1
    started = jnp.int32(0)
    for j in range(NS):
        start = STORED - slash[core, j]
        first = jnp.clip(chip * PER_CHIP - start, 0, 32)
        last = jnp.clip((chip + 1) * PER_CHIP - start, 0, 32)

        def one(block, count, j=j, start=start):
            lane = lane_of(slash, core, j, block, chip) - low
            take = (lane >= 0) & (lane < lanes)
            row = pl.multiple_of(((start + block) & (PER_CHIP - 1)) * BLOCK, BLOCK)
            slot = (plane_row(block) * lanes + lane) * 2
            to = member(block)

            @pl.when(take)
            def _():
                pltpu.make_async_copy(keys.at[pl.ds(row, BLOCK)], out.at[to, slot], sem).start()
                pltpu.make_async_copy(
                    values.at[pl.ds(row, BLOCK)], out.at[to, slot + 1], sem
                ).start()

            return count + jnp.where(take, 2, 0)

        started = lax.fori_loop(first, last, one, started)
    if vert:
        for v in range(NV):
            block = vertical[core, v]
            mine = (block >> 7) == chip
            row = pl.multiple_of((block & (PER_CHIP - 1)) * BLOCK, BLOCK)

            @pl.when(mine)
            def _(v=v, row=row):
                pltpu.make_async_copy(keys.at[pl.ds(row, BLOCK)], out.at[v, SLOTS - 2], sem).start()
                pltpu.make_async_copy(
                    values.at[pl.ds(row, BLOCK)], out.at[v, SLOTS - 1], sem
                ).start()

            started = started + jnp.where(mine, 2, 0)
    copy_tiles(sem, started, keys.at[pl.ds(0, BLOCK)])


def first_call(place, slash, vertical, keys, values, low, vert):
    slots = SLOTS if vert else 8

    def kernel(*refs):
        pack_first(*refs, low=low, vert=vert)

    return pl.pallas_call(
        kernel,
        out_shape=jax.ShapeDtypeStruct((8, slots, BLOCK, HD), jnp.bfloat16),
        in_specs=[SMEM, SMEM, SMEM, HBM, HBM],
        out_specs=HBM,
        scratch_shapes=[pltpu.SemaphoreType.DMA],
        name="pack_first" if vert else "pack_rest",
    )(place, slash, vertical, keys, values)


def pack_second(place, slash, vertical, *refs, rounds):
    got, out, sem = refs[:rounds], refs[rounds], refs[rounds + 1]
    chip, core = place[0], place[1]
    row_here = plane_row(chip)
    started = jnp.int32(0)
    for zh in range(4):
        block = (chip & 25) + zh * 2
        for j in range(NS):
            source = (STORED + block - slash[core, j]) >> 7
            lane = lane_of(slash, core, j, block, source)
            frm = member(source)
            mine = plane_row(source) == row_here
            if rounds == 1:
                choices = [(mine, got[0], (zh * LANES + lane) * 2)]
            else:
                choices = [
                    (mine & (lane < LANES), got[0], (zh * LANES + lane) * 2),
                    (mine & (lane >= LANES), got[1], zh * 2),
                ]
            for test, ref, slot in choices:

                @pl.when(test)
                def _(ref=ref, slot=slot, frm=frm, zh=zh, j=j):
                    pltpu.make_async_copy(
                        ref.at[frm, pl.ds(slot, 2)], out.at[zh, pl.ds(j * 2, 2)], sem
                    ).start()

            started = started + jnp.where(mine, 1, 0)
    source = vertical[core, member(chip)] >> 7
    mine = plane_row(source) == row_here
    for zh in range(4):

        @pl.when(mine)
        def _(zh=zh, frm=member(source)):
            pltpu.make_async_copy(
                got[0].at[frm, pl.ds(SLOTS - 2, 2)], out.at[zh, pl.ds(NS * 2, 2)], sem
            ).start()

    started = started + jnp.where(mine, 4, 0)
    copy_tiles(sem, started, out.at[0, pl.ds(0, 2)])


def second_call(place, slash, vertical, *got):
    def kernel(*refs):
        pack_second(*refs, rounds=len(got))

    return pl.pallas_call(
        kernel,
        out_shape=jax.ShapeDtypeStruct((4, SLOTS2, BLOCK, HD), jnp.bfloat16),
        in_specs=[SMEM, SMEM, SMEM] + [HBM] * len(got),
        out_specs=HBM,
        scratch_shapes=[pltpu.SemaphoreType.DMA],
        name="pack_second",
    )(place, slash, vertical, *got)


def pick_vertical(place, vertical, got, out, sem):
    chip, core = place[0], place[1]
    frm = plane_row(vertical[core, member(chip)] >> 7)
    copies = [
        pltpu.make_async_copy(got.at[frm, pl.ds(NS * 2, 2)], out.at[g], sem.at[g]) for g in range(8)
    ]
    for c in copies:
        c.start()
    for c in copies:
        c.wait()


def vertical_call(place, vertical, got):
    return pl.pallas_call(
        pick_vertical,
        out_shape=jax.ShapeDtypeStruct((8, 2, BLOCK, HD), jnp.bfloat16),
        in_specs=[SMEM, SMEM, HBM],
        out_specs=HBM,
        scratch_shapes=[pltpu.SemaphoreType.DMA((8,))],
        name="pick_vertical",
    )(place, vertical, got)


COLS = (NV + NS + 2) * BLOCK
CHUNK = 128


def attend(place, slash, vertical, queries, fresh, got, vert, out, keys, values):
    chip, core = place[0], place[1]
    for v in range(NV):
        keys[v * BLOCK : (v + 1) * BLOCK] = vert[v, 0]
        values[v * BLOCK : (v + 1) * BLOCK] = vert[v, 1]
    column = lax.broadcasted_iota(jnp.int32, (1, COLS), 1)
    allowed = column < (NV + NS) * BLOCK
    for j in range(NS):
        block = STORED + chip - slash[core, j]
        frm = plane_row(block >> 7)
        at = (NV + j) * BLOCK
        keys[at : at + BLOCK] = got[frm, 2 * j]
        values[at : at + BLOCK] = got[frm, 2 * j + 1]
        repeated = jnp.int32(0)
        for v in range(NV):
            repeated = repeated | jnp.where(vertical[core, v] == block, 1, 0)
        here = (column >= at) & (column < at + BLOCK)
        allowed = allowed & jnp.logical_not(here & (repeated == 1))
    at = (NV + NS) * BLOCK
    keys[at : at + BLOCK] = fresh[:, :HD]
    values[at : at + BLOCK] = fresh[:, HD:]
    keys[at + BLOCK :] = jnp.zeros((BLOCK, HD), jnp.bfloat16)
    values[at + BLOCK :] = jnp.zeros((BLOCK, HD), jnp.bfloat16)
    row = lax.broadcasted_iota(jnp.int32, (CHUNK, COLS), 0) & (BLOCK - 1)
    col = lax.broadcasted_iota(jnp.int32, (CHUNK, COLS), 1)
    own = (col >= at) & (col - at <= row) & (col < at + BLOCK)
    keep = jnp.where(own, 1, 0) + jnp.where(allowed, 1, 0)
    scale = 1.0 / math.sqrt(HD)
    for pair in range(GROUP * BLOCK // CHUNK):
        per = CHUNK // BLOCK
        q = jnp.concatenate(
            [
                queries[:, (pair * per + i) * HD : (pair * per + i + 1) * HD]
                for i in range(per)
            ],
            axis=0,
        )
        scores = lax.dot_general(
            q, keys[...], (((1,), (1,)), ((), ())), preferred_element_type=jnp.float32
        )
        scores = jnp.where(keep > 0, scores * scale, NEGATIVE)
        peak = jnp.max(scores, axis=-1, keepdims=True)
        weights = jnp.exp(scores - peak)
        total = jnp.sum(weights, axis=-1, keepdims=True)
        acc = jnp.dot(
            weights.astype(jnp.bfloat16), values[...], preferred_element_type=jnp.float32
        )
        result = (acc / total).astype(jnp.bfloat16)
        for i in range(per):
            cols = slice((pair * per + i) * HD, (pair * per + i + 1) * HD)
            for c in range(2):
                for y in range(4):
                    r = i * BLOCK + c * 32 + y * 8
                    out[y * 2 + c, :, cols] = result[r : r + 8]


def attend_call(place, slash, vertical, queries, fresh, got, vert):
    return pl.pallas_call(
        attend,
        out_shape=jax.ShapeDtypeStruct((8, 8, GROUP * HD), jnp.bfloat16),
        in_specs=[SMEM, SMEM, SMEM, VMEM, VMEM, VMEM, VMEM],
        out_specs=VMEM,
        scratch_shapes=[
            pltpu.VMEM((COLS, HD), jnp.bfloat16),
            pltpu.VMEM((COLS, HD), jnp.bfloat16),
        ],
        compiler_params=pltpu.CompilerParams(vmem_limit_bytes=32 * 1024 * 1024),
        name="attend",
    )(place, slash, vertical, queries, fresh, got, vert)


def too_many(slash):
    blocks = jnp.arange(32, dtype=jnp.int32)
    chips = (STORED + blocks[None, :] - slash[:, None]) >> 7
    same = jnp.sum((chips[:, None, :] == chips[None, :, :]).astype(jnp.int32), axis=1)
    return jnp.max(same) > LANES


def body(queries, cache_keys, cache_values, new_keys, new_values, vertical, slash):
    core = lax.axis_index("c").astype(jnp.int32)
    chip = (
        lax.axis_index("x") * 8 + lax.axis_index("zh") * 2 + lax.axis_index("zp")
    ).astype(jnp.int32)
    place = jnp.stack([chip, core])
    rows = queries.shape[0]
    mixed = jnp.concatenate(
        [
            queries.reshape(rows, 2, GROUP * HD),
            new_keys.reshape(rows, 2, HD),
            new_values.reshape(rows, 2, HD),
        ],
        axis=2,
    )
    mixed = lax.all_to_all(mixed, "c", 1, 0, tiled=True).reshape(2 * rows, GROUP * HD + 2 * HD)
    head_queries, fresh = mixed[:, : GROUP * HD], mixed[:, GROUP * HD :]
    keys = lax.all_to_all(cache_keys, "c", 1, 0, tiled=True)
    values = lax.all_to_all(cache_values, "c", 1, 0, tiled=True)

    sent = first_call(place, slash, vertical, keys, values, 0, True)
    got = lax.all_to_all(sent, ("x", "zp"), 0, 0, tiled=True)

    def more():
        rest = first_call(place, slash, vertical, keys, values, LANES, False)
        rest = lax.all_to_all(rest, ("x", "zp"), 0, 0, tiled=True)
        return second_call(place, slash, vertical, got, rest)

    def enough():
        return second_call(place, slash, vertical, got)

    sent = lax.cond(too_many(slash[core]), more, enough)
    got = lax.all_to_all(sent, "zh", 0, 0, tiled=True)
    vert = vertical_call(place, vertical, got)
    vert = lax.all_to_all(vert, ("x", "zp"), 0, 0, tiled=True)
    out = attend_call(place, slash, vertical, head_queries, fresh, got, vert)
    out = lax.all_to_all(out, ("y", "c"), 0, 0, tiled=True)
    return out.transpose(1, 0, 2).reshape(8, 8 * GROUP * HD)


def solution(mesh):
    parts = Mesh(mesh.devices.reshape(4, 4, 2, 2, 4), ("x", "zh", "zp", "c", "y"))
    ctx = ("x", "zh", "zp", "c")
    in_specs = (P(ctx, "y"),) * 5 + (P("y", None),) * 2
    out_specs = P(ctx + ("y",), None)
    return jax.shard_map(body, mesh=parts, in_specs=in_specs, out_specs=out_specs, check_vma=False)
```

```python
import math

import jax
import jax.numpy as jnp
from jax import lax
from jax.experimental import pallas as pl
from jax.experimental.pallas import tpu as pltpu
from jax.sharding import Mesh, PartitionSpec as P

HD = 128
BLOCK = 64
NV = 8
NS = 4
GROUP = 8
STORED = 4096
PER_CHIP = 128
LANES = 2
NEGATIVE = -1e30
SLOTS = 4 * LANES * 2
PARTS = 4
PART = BLOCK // PARTS
SWAP = 2 * STORED // 64 * BLOCK
OWN = 32

SMEM = pl.BlockSpec(memory_space=pltpu.SMEM)
HBM = pl.BlockSpec(memory_space=pl.ANY)
VMEM = pl.BlockSpec(memory_space=pltpu.VMEM)
PARAMS = pltpu.CompilerParams(vmem_limit_bytes=32 * 1024 * 1024)


def member(chip):
    return (chip >> 3) * 2 + (chip & 1)


def plane_row(chip):
    return (chip >> 1) & 3


def lane_of(slash, core, j, block, chip):
    rank = jnp.int32(0)
    for i in range(j):
        rank = rank + jnp.where((STORED + block - slash[core, i]) >> 7 == chip, 1, 0)
    return rank


def wait_for(sem, count, like):
    def one(_, carry):
        pltpu.make_async_copy(like, like, sem).wait()
        return carry

    lax.fori_loop(0, count, one, 0)


def pack_swap(place, cache_keys, cache_values, queries, new_keys, new_values, out, sem):
    other = 1 - place[1]
    cols = pl.ds(pl.multiple_of(other * HD, HD), HD)
    rows = cache_keys.shape[0]
    copies = [
        (cache_keys.at[:, cols], out.at[pl.ds(0, rows)]),
        (cache_values.at[:, cols], out.at[pl.ds(rows, rows)]),
        (new_keys.at[:, cols], out.at[pl.ds(SWAP + GROUP * OWN, OWN)]),
        (new_values.at[:, cols], out.at[pl.ds(SWAP + GROUP * OWN + OWN, OWN)]),
    ]
    for g in range(GROUP):
        at = pl.multiple_of((other * GROUP + g) * HD, HD)
        copies.append((queries.at[:, pl.ds(at, HD)], out.at[pl.ds(SWAP + g * OWN, OWN)]))
    copies = [pltpu.make_async_copy(a, b, sem.at[i]) for i, (a, b) in enumerate(copies)]
    for c in copies:
        c.start()
    for c in copies:
        c.wait()


def swap_call(place, *arrays):
    return pl.pallas_call(
        pack_swap,
        out_shape=jax.ShapeDtypeStruct((SWAP + GROUP * OWN + 2 * OWN, HD), jnp.bfloat16),
        in_specs=[SMEM] + [HBM] * 5,
        out_specs=VMEM,
        scratch_shapes=[pltpu.SemaphoreType.DMA((4 + GROUP,))],
        compiler_params=PARAMS,
        name="pack_swap",
    )(place, *arrays)


def cached_block(core, block, cache_keys, cache_values, swapped, act):
    local = pl.ds(pl.multiple_of((block & 63) * BLOCK, BLOCK), BLOCK)
    cols = pl.ds(pl.multiple_of(core * HD, HD), HD)
    here = ((block >> 6) & 1) == core

    @pl.when(here)
    def _():
        act(cache_keys.at[local, cols], cache_values.at[local, cols])

    @pl.when(jnp.logical_not(here))
    def _():
        row = pl.multiple_of((block & 63) * BLOCK, BLOCK)
        act(swapped.at[pl.ds(row, BLOCK)], swapped.at[pl.ds(row + SWAP // 2, BLOCK)])


def pack_first(place, slash, cache_keys, cache_values, swapped, out, sem, *, low, lanes):
    chip, core = place[0], place[1]
    started = jnp.int32(0)
    for j in range(NS):
        start = STORED - slash[core, j]
        first = jnp.clip(chip * PER_CHIP - start, 0, 32)
        last = jnp.clip((chip + 1) * PER_CHIP - start, 0, 32)

        def one(block, count, j=j, start=start):
            lane = lane_of(slash, core, j, block, chip) - low
            take = (lane >= 0) & (lane < lanes)
            slot = (plane_row(block) * lanes + lane) * 2
            to = member(block)

            def act(key_rows, value_rows):
                pltpu.make_async_copy(key_rows, out.at[to, slot], sem).start()
                pltpu.make_async_copy(value_rows, out.at[to, slot + 1], sem).start()

            @pl.when(take)
            def _():
                cached_block(core, start + block, cache_keys, cache_values, swapped, act)

            return count + jnp.where(take, 2, 0)

        started = lax.fori_loop(first, last, one, started)
    wait_for(sem, started, out.at[0, 0])


def first_call(place, slash, cache_keys, cache_values, swapped, low, lanes):
    def kernel(*refs):
        pack_first(*refs, low=low, lanes=lanes)

    return pl.pallas_call(
        kernel,
        out_shape=jax.ShapeDtypeStruct((8, 4 * lanes * 2, BLOCK, HD), jnp.bfloat16),
        in_specs=[SMEM, SMEM, HBM, HBM, HBM],
        out_specs=VMEM,
        scratch_shapes=[pltpu.SemaphoreType.DMA],
        compiler_params=PARAMS,
        name="pack_rest" if low else "pack_first",
    )(place, slash, cache_keys, cache_values, swapped)


def pack_vertical(place, vertical, cache_keys, cache_values, swapped, out, sem):
    chip, core = place[0], place[1]
    started = jnp.int32(0)
    for v in range(NV):
        block = vertical[core, v]
        mine = (block >> 7) == chip

        def act(key_rows, value_rows, v=v):
            for p in range(PARTS):
                some = pl.ds(p * PART, PART)
                pltpu.make_async_copy(key_rows.at[some], out.at[v * PARTS + p, 0], sem).start()
                pltpu.make_async_copy(value_rows.at[some], out.at[v * PARTS + p, 1], sem).start()

        @pl.when(mine)
        def _(block=block, act=act):
            cached_block(core, block, cache_keys, cache_values, swapped, act)

        started = started + jnp.where(mine, 2 * PARTS, 0)
    wait_for(sem, started, out.at[0, 0])


def vertical_call(place, vertical, cache_keys, cache_values, swapped):
    return pl.pallas_call(
        pack_vertical,
        out_shape=jax.ShapeDtypeStruct((NV * PARTS, 2, PART, HD), jnp.bfloat16),
        in_specs=[SMEM, SMEM, HBM, HBM, HBM],
        out_specs=VMEM,
        scratch_shapes=[pltpu.SemaphoreType.DMA],
        compiler_params=PARAMS,
        name="pack_vertical",
    )(place, vertical, cache_keys, cache_values, swapped)


def spread_vertical(place, vertical, got, out):
    chip, core = place[0], place[1]
    mine = got[vertical[core, chip >> 2] >> 7]
    for to in range(NV * PARTS):
        out[to] = mine


def spread_call(place, vertical, got):
    return pl.pallas_call(
        spread_vertical,
        out_shape=jax.ShapeDtypeStruct((NV * PARTS, 2, PART, HD), jnp.bfloat16),
        in_specs=[SMEM, SMEM, VMEM],
        out_specs=VMEM,
        compiler_params=PARAMS,
        name="spread_vertical",
    )(place, vertical, got)


def pack_second(place, slash, *refs, rounds):
    got, out, sem = refs[:rounds], refs[rounds], refs[rounds + 1]
    chip, core = place[0], place[1]
    row_here = plane_row(chip)
    started = jnp.int32(0)
    for zh in range(4):
        block = (chip & 25) + zh * 2
        for j in range(NS):
            source = (STORED + block - slash[core, j]) >> 7
            lane = lane_of(slash, core, j, block, source)
            frm = member(source)
            mine = plane_row(source) == row_here
            if rounds == 1:
                choices = [(mine, got[0], (zh * LANES + lane) * 2)]
            else:
                choices = [
                    (mine & (lane < LANES), got[0], (zh * LANES + lane) * 2),
                    (mine & (lane >= LANES), got[1], zh * 2),
                ]
            for test, ref, slot in choices:

                @pl.when(test)
                def _(ref=ref, slot=slot, frm=frm, zh=zh, j=j):
                    pltpu.make_async_copy(
                        ref.at[frm, pl.ds(slot, 2)], out.at[zh, pl.ds(j * 2, 2)], sem
                    ).start()

            started = started + jnp.where(mine, 1, 0)
    wait_for(sem, started, out.at[0, pl.ds(0, 2)])


def second_call(place, slash, *got):
    def kernel(*refs):
        pack_second(*refs, rounds=len(got))

    return pl.pallas_call(
        kernel,
        out_shape=jax.ShapeDtypeStruct((4, NS * 2, BLOCK, HD), jnp.bfloat16),
        in_specs=[SMEM, SMEM] + [HBM] * len(got),
        out_specs=VMEM,
        scratch_shapes=[pltpu.SemaphoreType.DMA],
        compiler_params=PARAMS,
        name="pack_second",
    )(place, slash, *got)


COLS = (NV + NS + 2) * BLOCK
CHUNK = 128


def attend(
    place, slash, vertical, queries, new_keys, new_values, swapped, got, vert, out,
    keys, values, rows, sem,
):
    chip, core = place[0], place[1]
    theirs = pltpu.make_async_copy(swapped.at[pl.ds(SWAP, (GROUP + 2) * OWN)], rows.at[1], sem)
    theirs.start()
    for v in range(NV):
        for p in range(PARTS):
            at = v * BLOCK + p * PART
            keys[at : at + PART] = vert[v * PARTS + p, 0]
            values[at : at + PART] = vert[v * PARTS + p, 1]
    column = lax.broadcasted_iota(jnp.int32, (1, COLS), 1)
    allowed = column < (NV + NS) * BLOCK
    for j in range(NS):
        block = STORED + chip - slash[core, j]
        frm = plane_row(block >> 7)
        at = (NV + j) * BLOCK
        keys[at : at + BLOCK] = got[frm, 2 * j]
        values[at : at + BLOCK] = got[frm, 2 * j + 1]
        repeated = jnp.int32(0)
        for v in range(NV):
            repeated = repeated | jnp.where(vertical[core, v] == block, 1, 0)
        here = (column >= at) & (column < at + BLOCK)
        allowed = allowed & jnp.logical_not(here & (repeated == 1))
    for g in range(GROUP):
        cols = pl.ds(pl.multiple_of((core * GROUP + g) * HD, HD), HD)
        rows[0, g * OWN : (g + 1) * OWN] = queries[:, cols]
    theirs.wait()
    at = (NV + NS) * BLOCK
    mine = pl.ds(pl.multiple_of(core * OWN, OWN) + at, OWN)
    rest = pl.ds(pl.multiple_of((1 - core) * OWN, OWN) + at, OWN)
    cols = pl.ds(pl.multiple_of(core * HD, HD), HD)
    keys[mine] = new_keys[:, cols]
    values[mine] = new_values[:, cols]
    keys[rest] = rows[1, GROUP * OWN : (GROUP + 1) * OWN]
    values[rest] = rows[1, (GROUP + 1) * OWN :]
    keys[at + BLOCK :] = jnp.zeros((BLOCK, HD), jnp.bfloat16)
    values[at + BLOCK :] = jnp.zeros((BLOCK, HD), jnp.bfloat16)
    row = lax.broadcasted_iota(jnp.int32, (CHUNK, COLS), 0) & (BLOCK - 1)
    col = lax.broadcasted_iota(jnp.int32, (CHUNK, COLS), 1)
    own = (col >= at) & (col - at <= row) & (col < at + BLOCK)
    keep = jnp.where(own, 1, 0) + jnp.where(allowed, 1, 0)
    scale = 1.0 / math.sqrt(HD)
    per = CHUNK // BLOCK
    for pair in range(GROUP // per):
        parts = []
        for i in range(per):
            g = pair * per + i
            parts += [
                rows[pl.ds(core, 1), g * OWN : (g + 1) * OWN][0],
                rows[pl.ds(1 - core, 1), g * OWN : (g + 1) * OWN][0],
            ]
        q = jnp.concatenate(parts, axis=0)
        scores = lax.dot_general(
            q, keys[...], (((1,), (1,)), ((), ())), preferred_element_type=jnp.float32
        )
        scores = jnp.where(keep > 0, scores * scale, NEGATIVE)
        peak = jnp.max(scores, axis=-1, keepdims=True)
        weights = jnp.exp(scores - peak)
        total = jnp.sum(weights, axis=-1, keepdims=True)
        acc = jnp.dot(
            weights.astype(jnp.bfloat16), values[...], preferred_element_type=jnp.float32
        )
        result = (acc / total).astype(jnp.bfloat16)
        for i in range(per):
            cols = slice((pair * per + i) * HD, (pair * per + i + 1) * HD)
            for c in range(2):
                for y in range(4):
                    r = i * BLOCK + c * 32 + y * 8
                    out[y * 2 + c, :, cols] = result[r : r + 8]


def attend_call(place, slash, vertical, queries, new_keys, new_values, swapped, got, vert):
    return pl.pallas_call(
        attend,
        out_shape=jax.ShapeDtypeStruct((8, 8, GROUP * HD), jnp.bfloat16),
        in_specs=[SMEM, SMEM, SMEM, VMEM, VMEM, VMEM, HBM, VMEM, VMEM],
        out_specs=VMEM,
        scratch_shapes=[
            pltpu.VMEM((COLS, HD), jnp.bfloat16),
            pltpu.VMEM((COLS, HD), jnp.bfloat16),
            pltpu.VMEM((2, (GROUP + 2) * OWN, HD), jnp.bfloat16),
            pltpu.SemaphoreType.DMA,
        ],
        compiler_params=PARAMS,
        name="attend",
    )(place, slash, vertical, queries, new_keys, new_values, swapped, got, vert)


def too_many(slash):
    blocks = jnp.arange(32, dtype=jnp.int32)
    chips = (STORED + blocks[None, :] - slash[:, None]) >> 7
    same = jnp.sum((chips[:, None, :] == chips[None, :, :]).astype(jnp.int32), axis=1)
    return jnp.max(same) > LANES


def body(queries, cache_keys, cache_values, new_keys, new_values, vertical, slash):
    core = lax.axis_index("c").astype(jnp.int32)
    chip = (
        lax.axis_index("x") * 8 + lax.axis_index("zh") * 2 + lax.axis_index("zp")
    ).astype(jnp.int32)
    place = jnp.stack([chip, core])
    own = swap_call(place, cache_keys, cache_values, queries, new_keys, new_values)
    swapped = lax.ppermute(own, "c", [(0, 1), (1, 0)])
    cached = (cache_keys, cache_values, swapped)
    chips = ("x", "zh", "zp")

    sent = first_call(place, slash, *cached, 0, LANES)
    got = lax.all_to_all(sent, ("x", "zp"), 0, 0, tiled=True)
    vert = vertical_call(place, vertical, *cached)
    vert = lax.all_to_all(vert, chips, 0, 0, tiled=True)
    vert = spread_call(place, vertical, vert)
    vert = lax.all_to_all(vert, chips, 0, 0, tiled=True)

    def more():
        rest = first_call(place, slash, *cached, LANES, 1)
        rest = lax.all_to_all(rest, ("x", "zp"), 0, 0, tiled=True)
        return second_call(place, slash, got, rest)

    def enough():
        return second_call(place, slash, got)

    sent = lax.cond(too_many(slash[core]), more, enough)
    got = lax.all_to_all(sent, "zh", 0, 0, tiled=True)
    out = attend_call(
        place, slash, vertical, queries, new_keys, new_values, swapped, got, vert
    )
    out = lax.all_to_all(out, ("y", "c"), 0, 0, tiled=True)
    return out.transpose(1, 0, 2).reshape(8, 8 * GROUP * HD)


def solution(mesh):
    parts = Mesh(mesh.devices.reshape(4, 4, 2, 2, 4), ("x", "zh", "zp", "c", "y"))
    ctx = ("x", "zh", "zp", "c")
    in_specs = (P(ctx, "y"),) * 5 + (P("y", None),) * 2
    out_specs = P(ctx + ("y",), None)
    return jax.shard_map(body, mesh=parts, in_specs=in_specs, out_specs=out_specs, check_vma=False)
```

```python
import math

import jax
import jax.numpy as jnp
from jax import lax
from jax.experimental import pallas as pl
from jax.experimental.pallas import tpu as pltpu
from jax.sharding import Mesh, PartitionSpec as P

HD = 128
BLOCK = 64
NV = 8
NS = 4
GROUP = 8
STORED = 4096
PER_CHIP = 128
LANES = 2
NEGATIVE = -1e30
SLOTS = 4 * LANES * 2 + 2
SLOTS2 = NS * 2 + 2
SWAP = 2 * STORED // 64 * BLOCK
OWN = 32

SMEM = pl.BlockSpec(memory_space=pltpu.SMEM)
ANY = pl.BlockSpec(memory_space=pl.ANY)
HBM = pl.BlockSpec(memory_space=pltpu.HBM)
VMEM = pl.BlockSpec(memory_space=pltpu.VMEM)
PARAMS = pltpu.CompilerParams(vmem_limit_bytes=32 * 1024 * 1024)


def member(chip):
    return (chip >> 3) * 2 + (chip & 1)


def plane_row(chip):
    return (chip >> 1) & 3


def lane_of(slash, core, j, block, chip):
    rank = jnp.int32(0)
    for i in range(j):
        rank = rank + jnp.where((STORED + block - slash[core, i]) >> 7 == chip, 1, 0)
    return rank


def wait_for(sem, count, like):
    def one(_, carry):
        pltpu.make_async_copy(like, like, sem).wait()
        return carry

    lax.fori_loop(0, count, one, 0)


def pack_swap(place, cache_keys, cache_values, queries, new_keys, new_values, out, sem):
    other = 1 - place[1]
    cols = pl.ds(pl.multiple_of(other * HD, HD), HD)
    rows = cache_keys.shape[0]
    copies = [
        (cache_keys.at[:, cols], out.at[pl.ds(0, rows)]),
        (cache_values.at[:, cols], out.at[pl.ds(rows, rows)]),
        (new_keys.at[:, cols], out.at[pl.ds(SWAP + GROUP * OWN, OWN)]),
        (new_values.at[:, cols], out.at[pl.ds(SWAP + GROUP * OWN + OWN, OWN)]),
    ]
    for g in range(GROUP):
        at = pl.multiple_of((other * GROUP + g) * HD, HD)
        copies.append((queries.at[:, pl.ds(at, HD)], out.at[pl.ds(SWAP + g * OWN, OWN)]))
    copies = [pltpu.make_async_copy(a, b, sem.at[i]) for i, (a, b) in enumerate(copies)]
    for c in copies:
        c.start()
    for c in copies:
        c.wait()


def swap_call(place, *arrays):
    return pl.pallas_call(
        pack_swap,
        out_shape=jax.ShapeDtypeStruct((SWAP + GROUP * OWN + 2 * OWN, HD), jnp.bfloat16),
        in_specs=[SMEM] + [HBM] * 5,
        out_specs=VMEM,
        scratch_shapes=[pltpu.SemaphoreType.DMA((4 + GROUP,))],
        compiler_params=PARAMS,
        name="pack_swap",
    )(place, *arrays)


def cached_block(core, block, cache_keys, cache_values, swapped, act):
    local = pl.ds(pl.multiple_of((block & 63) * BLOCK, BLOCK), BLOCK)
    cols = pl.ds(pl.multiple_of(core * HD, HD), HD)
    here = ((block >> 6) & 1) == core

    @pl.when(here)
    def _():
        act(cache_keys.at[local, cols], cache_values.at[local, cols])

    @pl.when(jnp.logical_not(here))
    def _():
        row = pl.multiple_of((block & 63) * BLOCK, BLOCK)
        act(swapped.at[pl.ds(row, BLOCK)], swapped.at[pl.ds(row + SWAP // 2, BLOCK)])


def pack_first(
    place, slash, vertical, cache_keys, cache_values, swapped, out, sem, *, low, lanes
):
    chip, core = place[0], place[1]
    started = jnp.int32(0)
    for j in range(NS):
        start = STORED - slash[core, j]
        first = jnp.clip(chip * PER_CHIP - start, 0, 32)
        last = jnp.clip((chip + 1) * PER_CHIP - start, 0, 32)

        def one(block, count, j=j, start=start):
            lane = lane_of(slash, core, j, block, chip) - low
            take = (lane >= 0) & (lane < lanes)
            slot = (plane_row(block) * lanes + lane) * 2
            to = member(block)

            def act(key_rows, value_rows):
                pltpu.make_async_copy(key_rows, out.at[to, slot], sem).start()
                pltpu.make_async_copy(value_rows, out.at[to, slot + 1], sem).start()

            @pl.when(take)
            def _():
                cached_block(core, start + block, cache_keys, cache_values, swapped, act)

            return count + jnp.where(take, 2, 0)

        started = lax.fori_loop(first, last, one, started)
    for v in range(0 if low else NV):
        block = vertical[core, v]
        mine = (block >> 7) == chip

        def act(key_rows, value_rows, v=v):
            pltpu.make_async_copy(key_rows, out.at[v, SLOTS - 2], sem).start()
            pltpu.make_async_copy(value_rows, out.at[v, SLOTS - 1], sem).start()

        @pl.when(mine)
        def _(block=block, act=act):
            cached_block(core, block, cache_keys, cache_values, swapped, act)

        started = started + jnp.where(mine, 2, 0)
    wait_for(sem, started, out.at[0, 0])


def first_call(place, slash, vertical, cache_keys, cache_values, swapped, low, lanes):
    slots = 4 * lanes * 2 + (0 if low else 2)

    def kernel(*refs):
        pack_first(*refs, low=low, lanes=lanes)

    return pl.pallas_call(
        kernel,
        out_shape=jax.ShapeDtypeStruct((8, slots, BLOCK, HD), jnp.bfloat16),
        in_specs=[SMEM, SMEM, SMEM, ANY, ANY, ANY],
        out_specs=VMEM,
        scratch_shapes=[pltpu.SemaphoreType.DMA],
        compiler_params=PARAMS,
        name="pack_rest" if low else "pack_first",
    )(place, slash, vertical, cache_keys, cache_values, swapped)


def spread_vertical(place, vertical, got, out):
    chip, core = place[0], place[1]
    mine = got[plane_row(vertical[core, member(chip)] >> 7), NS * 2 :]
    for to in range(NV):
        out[to] = mine


def spread_call(place, vertical, got):
    return pl.pallas_call(
        spread_vertical,
        out_shape=jax.ShapeDtypeStruct((NV, 2, BLOCK, HD), jnp.bfloat16),
        in_specs=[SMEM, SMEM, VMEM],
        out_specs=VMEM,
        compiler_params=PARAMS,
        name="spread_vertical",
    )(place, vertical, got)


def pack_second(place, slash, vertical, *refs, rounds):
    got, out, sem = refs[:rounds], refs[rounds], refs[rounds + 1]
    chip, core = place[0], place[1]
    row_here = plane_row(chip)
    started = jnp.int32(0)
    for zh in range(4):
        block = (chip & 25) + zh * 2
        for j in range(NS):
            source = (STORED + block - slash[core, j]) >> 7
            lane = lane_of(slash, core, j, block, source)
            frm = member(source)
            mine = plane_row(source) == row_here
            if rounds == 1:
                choices = [(mine, got[0], (zh * LANES + lane) * 2)]
            else:
                choices = [
                    (mine & (lane < LANES), got[0], (zh * LANES + lane) * 2),
                    (mine & (lane >= LANES), got[1], zh * 2),
                ]
            for test, ref, slot in choices:

                @pl.when(test)
                def _(ref=ref, slot=slot, frm=frm, zh=zh, j=j):
                    pltpu.make_async_copy(
                        ref.at[frm, pl.ds(slot, 2)], out.at[zh, pl.ds(j * 2, 2)], sem
                    ).start()

            started = started + jnp.where(mine, 1, 0)
    source = vertical[core, member(chip)] >> 7
    mine = plane_row(source) == row_here
    for zh in range(4):

        @pl.when(mine)
        def _(zh=zh, frm=member(source)):
            pltpu.make_async_copy(
                got[0].at[frm, pl.ds(SLOTS - 2, 2)], out.at[zh, pl.ds(NS * 2, 2)], sem
            ).start()

    started = started + jnp.where(mine, 4, 0)
    wait_for(sem, started, out.at[0, pl.ds(0, 2)])


def second_call(place, slash, vertical, *got):
    def kernel(*refs):
        pack_second(*refs, rounds=len(got))

    return pl.pallas_call(
        kernel,
        out_shape=jax.ShapeDtypeStruct((4, SLOTS2, BLOCK, HD), jnp.bfloat16),
        in_specs=[SMEM, SMEM, SMEM] + [ANY] * len(got),
        out_specs=VMEM,
        scratch_shapes=[pltpu.SemaphoreType.DMA],
        compiler_params=PARAMS,
        name="pack_second",
    )(place, slash, vertical, *got)


COLS = (NV + NS + 2) * BLOCK
CHUNK = 128


def attend(
    place, slash, vertical, queries, new_keys, new_values, swapped, got, vert, out,
    keys, values, rows, sem,
):
    chip, core = place[0], place[1]
    theirs = pltpu.make_async_copy(swapped.at[pl.ds(SWAP, (GROUP + 2) * OWN)], rows.at[1], sem)
    theirs.start()
    for v in range(NV):
        keys[v * BLOCK : (v + 1) * BLOCK] = vert[v, 0]
        values[v * BLOCK : (v + 1) * BLOCK] = vert[v, 1]
    column = lax.broadcasted_iota(jnp.int32, (1, COLS), 1)
    allowed = column < (NV + NS) * BLOCK
    for j in range(NS):
        block = STORED + chip - slash[core, j]
        frm = plane_row(block >> 7)
        at = (NV + j) * BLOCK
        keys[at : at + BLOCK] = got[frm, 2 * j]
        values[at : at + BLOCK] = got[frm, 2 * j + 1]
        repeated = jnp.int32(0)
        for v in range(NV):
            repeated = repeated | jnp.where(vertical[core, v] == block, 1, 0)
        here = (column >= at) & (column < at + BLOCK)
        allowed = allowed & jnp.logical_not(here & (repeated == 1))
    for g in range(GROUP):
        cols = pl.ds(pl.multiple_of((core * GROUP + g) * HD, HD), HD)
        rows[0, g * OWN : (g + 1) * OWN] = queries[:, cols]
    theirs.wait()
    at = (NV + NS) * BLOCK
    mine = pl.ds(pl.multiple_of(core * OWN, OWN) + at, OWN)
    rest = pl.ds(pl.multiple_of((1 - core) * OWN, OWN) + at, OWN)
    cols = pl.ds(pl.multiple_of(core * HD, HD), HD)
    keys[mine] = new_keys[:, cols]
    values[mine] = new_values[:, cols]
    keys[rest] = rows[1, GROUP * OWN : (GROUP + 1) * OWN]
    values[rest] = rows[1, (GROUP + 1) * OWN :]
    keys[at + BLOCK :] = jnp.zeros((BLOCK, HD), jnp.bfloat16)
    values[at + BLOCK :] = jnp.zeros((BLOCK, HD), jnp.bfloat16)
    row = lax.broadcasted_iota(jnp.int32, (CHUNK, COLS), 0) & (BLOCK - 1)
    col = lax.broadcasted_iota(jnp.int32, (CHUNK, COLS), 1)
    own = (col >= at) & (col - at <= row) & (col < at + BLOCK)
    keep = jnp.where(own, 1, 0) + jnp.where(allowed, 1, 0)
    scale = 1.0 / math.sqrt(HD)
    per = CHUNK // BLOCK
    for pair in range(GROUP // per):
        parts = []
        for i in range(per):
            g = pair * per + i
            parts += [
                rows[pl.ds(core, 1), g * OWN : (g + 1) * OWN][0],
                rows[pl.ds(1 - core, 1), g * OWN : (g + 1) * OWN][0],
            ]
        q = jnp.concatenate(parts, axis=0)
        scores = lax.dot_general(
            q, keys[...], (((1,), (1,)), ((), ())), preferred_element_type=jnp.float32
        )
        scores = jnp.where(keep > 0, scores * scale, NEGATIVE)
        peak = jnp.max(scores, axis=-1, keepdims=True)
        weights = jnp.exp(scores - peak)
        total = jnp.sum(weights, axis=-1, keepdims=True)
        acc = jnp.dot(
            weights.astype(jnp.bfloat16), values[...], preferred_element_type=jnp.float32
        )
        result = (acc / total).astype(jnp.bfloat16)
        for i in range(per):
            cols = slice((pair * per + i) * HD, (pair * per + i + 1) * HD)
            for c in range(2):
                for y in range(4):
                    r = i * BLOCK + c * 32 + y * 8
                    out[y * 2 + c, :, cols] = result[r : r + 8]


def attend_call(place, slash, vertical, queries, new_keys, new_values, swapped, got, vert):
    return pl.pallas_call(
        attend,
        out_shape=jax.ShapeDtypeStruct((8, 8, GROUP * HD), jnp.bfloat16),
        in_specs=[SMEM, SMEM, SMEM, VMEM, VMEM, VMEM, ANY, VMEM, VMEM],
        out_specs=VMEM,
        scratch_shapes=[
            pltpu.VMEM((COLS, HD), jnp.bfloat16),
            pltpu.VMEM((COLS, HD), jnp.bfloat16),
            pltpu.VMEM((2, (GROUP + 2) * OWN, HD), jnp.bfloat16),
            pltpu.SemaphoreType.DMA,
        ],
        compiler_params=PARAMS,
        name="attend",
    )(place, slash, vertical, queries, new_keys, new_values, swapped, got, vert)


def too_many(slash):
    blocks = jnp.arange(32, dtype=jnp.int32)
    chips = (STORED + blocks[None, :] - slash[:, None]) >> 7
    same = jnp.sum((chips[:, None, :] == chips[None, :, :]).astype(jnp.int32), axis=1)
    return jnp.max(same) > LANES


def body(queries, cache_keys, cache_values, new_keys, new_values, vertical, slash):
    core = lax.axis_index("c").astype(jnp.int32)
    chip = (
        lax.axis_index("x") * 8 + lax.axis_index("zh") * 2 + lax.axis_index("zp")
    ).astype(jnp.int32)
    place = jnp.stack([chip, core])
    own = swap_call(place, cache_keys, cache_values, queries, new_keys, new_values)
    swapped = lax.ppermute(own, "c", [(0, 1), (1, 0)])
    cached = (cache_keys, cache_values, swapped)
    sent = first_call(place, slash, vertical, *cached, 0, LANES)
    got = lax.all_to_all(sent, ("x", "zp"), 0, 0, tiled=True)

    def more():
        rest = first_call(place, slash, vertical, *cached, LANES, 1)
        rest = lax.all_to_all(rest, ("x", "zp"), 0, 0, tiled=True)
        return second_call(place, slash, vertical, got, rest)

    def enough():
        return second_call(place, slash, vertical, got)

    sent = lax.cond(too_many(slash[core]), more, enough)
    got = lax.all_to_all(sent, "zh", 0, 0, tiled=True)
    vert = spread_call(place, vertical, got)
    vert = lax.all_to_all(vert, ("x", "zp"), 0, 0, tiled=True)
    out = attend_call(
        place, slash, vertical, queries, new_keys, new_values, swapped, got, vert
    )
    out = lax.all_to_all(out, ("y", "c"), 0, 0, tiled=True)
    return out.transpose(1, 0, 2).reshape(8, 8 * GROUP * HD)


def solution(mesh):
    parts = Mesh(mesh.devices.reshape(4, 4, 2, 2, 4), ("x", "zh", "zp", "c", "y"))
    ctx = ("x", "zh", "zp", "c")
    in_specs = (P(ctx, "y"),) * 5 + (P("y", None),) * 2
    out_specs = P(ctx + ("y",), None)
    return jax.shard_map(body, mesh=parts, in_specs=in_specs, out_specs=out_specs, check_vma=False)
```

```python
import math

import jax
import jax.numpy as jnp
from jax import lax
from jax.experimental import pallas as pl
from jax.experimental.pallas import tpu as pltpu
from jax.sharding import Mesh, PartitionSpec as P

HD = 128
BLOCK = 64
NV = 8
NS = 4
GROUP = 8
STORED = 4096
PER_CHIP = 128
LANES = 2
NEGATIVE = -1e30
SLOTS = 4 * LANES * 2 + 2
SLOTS2 = (NS - 1) * 2 + 2
SWAP = 2 * STORED // 64 * BLOCK
OWN = 32

SMEM = pl.BlockSpec(memory_space=pltpu.SMEM)
ANY = pl.BlockSpec(memory_space=pl.ANY)
HBM = pl.BlockSpec(memory_space=pltpu.HBM)
VMEM = pl.BlockSpec(memory_space=pltpu.VMEM)
PARAMS = pltpu.CompilerParams(vmem_limit_bytes=32 * 1024 * 1024)


def offset(info, j):
    return info[2 + info[1] * NS + j]


def vertical_block(info, v):
    return info[2 + 2 * NS + info[1] * NV + v]


def slot_of(info, j):
    slot = jnp.int32(0)
    for i in range(j):
        other = offset(info, i)
        slot = slot + jnp.where((other == 32) | (other == STORED), 0, 1)
    mine = offset(info, j)
    return jnp.where((mine == 32) | (mine == STORED), NS - 2, slot)


def member(chip):
    return (chip >> 3) * 2 + (chip & 1)


def plane_row(chip):
    return (chip >> 1) & 3


def lane_of(info, j, block, chip):
    rank = jnp.int32(0)
    for i in range(j):
        rank = rank + jnp.where((STORED + block - offset(info, i)) >> 7 == chip, 1, 0)
    return rank


def wait_for(sem, count, like):
    def one(_, carry):
        pltpu.make_async_copy(like, like, sem).wait()
        return carry

    lax.fori_loop(0, count, one, 0)


def pack_swap(info, cache_keys, cache_values, queries, new_keys, new_values, out, kept, sem):
    rows = cache_keys.shape[0]
    copies = []
    for to, core, base in ((out, 1 - info[1], SWAP), (kept, info[1], 0)):
        cols = pl.ds(pl.multiple_of(core * HD, HD), HD)
        if base:
            copies.append((cache_keys.at[:, cols], to.at[pl.ds(0, rows)]))
            copies.append((cache_values.at[:, cols], to.at[pl.ds(rows, rows)]))
        for g in range(GROUP):
            at = pl.multiple_of((core * GROUP + g) * HD, HD)
            copies.append((queries.at[:, pl.ds(at, HD)], to.at[pl.ds(base + g * OWN, OWN)]))
        base = base + GROUP * OWN
        copies.append((new_keys.at[:, cols], to.at[pl.ds(base, OWN)]))
        copies.append((new_values.at[:, cols], to.at[pl.ds(base + OWN, OWN)]))
    copies = [pltpu.make_async_copy(a, b, sem.at[i]) for i, (a, b) in enumerate(copies)]
    for c in copies:
        c.start()
    for c in copies:
        c.wait()


def swap_call(info, *arrays):
    small = (GROUP + 2) * OWN
    return pl.pallas_call(
        pack_swap,
        out_shape=(
            jax.ShapeDtypeStruct((SWAP + small, HD), jnp.bfloat16),
            jax.ShapeDtypeStruct((small, HD), jnp.bfloat16),
        ),
        in_specs=[SMEM] + [HBM] * 5,
        out_specs=(VMEM, VMEM),
        scratch_shapes=[pltpu.SemaphoreType.DMA((2 + 2 * (GROUP + 2),))],
        compiler_params=PARAMS,
        name="pack_swap",
    )(info, *arrays)


def cached_block(core, block, cache_keys, cache_values, swapped, act):
    local = pl.ds(pl.multiple_of((block & 63) * BLOCK, BLOCK), BLOCK)
    cols = pl.ds(pl.multiple_of(core * HD, HD), HD)
    here = ((block >> 6) & 1) == core

    @pl.when(here)
    def _():
        act(cache_keys.at[local, cols], cache_values.at[local, cols])

    @pl.when(jnp.logical_not(here))
    def _():
        row = pl.multiple_of((block & 63) * BLOCK, BLOCK)
        act(swapped.at[pl.ds(row, BLOCK)], swapped.at[pl.ds(row + SWAP // 2, BLOCK)])


def pack_first(
    info, cache_keys, cache_values, swapped, out, sem, *, low, lanes
):
    chip, core = info[0], info[1]
    started = jnp.int32(0)
    for j in range(NS):
        start = STORED - offset(info, j)
        first = jnp.clip(chip * PER_CHIP - start, 0, 32)
        last = jnp.clip((chip + 1) * PER_CHIP - start, 0, 32)

        def one(block, count, j=j, start=start):
            lane = lane_of(info, j, block, chip) - low
            take = (lane >= 0) & (lane < lanes)
            slot = (plane_row(block) * lanes + lane) * 2
            to = member(block)

            def act(key_rows, value_rows):
                pltpu.make_async_copy(key_rows, out.at[to, slot], sem).start()
                pltpu.make_async_copy(value_rows, out.at[to, slot + 1], sem).start()

            @pl.when(take)
            def _():
                cached_block(core, start + block, cache_keys, cache_values, swapped, act)

            return count + jnp.where(take, 2, 0)

        started = lax.fori_loop(first, last, one, started)
    for v in range(0 if low else NV):
        block = vertical_block(info, v)
        mine = (block >> 7) == chip

        def act(key_rows, value_rows, v=v):
            pltpu.make_async_copy(key_rows, out.at[v, SLOTS - 2], sem).start()
            pltpu.make_async_copy(value_rows, out.at[v, SLOTS - 1], sem).start()

        @pl.when(mine)
        def _(block=block, act=act):
            cached_block(core, block, cache_keys, cache_values, swapped, act)

        started = started + jnp.where(mine, 2, 0)
    wait_for(sem, started, out.at[0, 0])


def first_call(info, cache_keys, cache_values, swapped, low, lanes):
    slots = 4 * lanes * 2 + (0 if low else 2)

    def kernel(*refs):
        pack_first(*refs, low=low, lanes=lanes)

    return pl.pallas_call(
        kernel,
        out_shape=jax.ShapeDtypeStruct((8, slots, BLOCK, HD), jnp.bfloat16),
        in_specs=[SMEM, HBM, HBM, ANY],
        out_specs=VMEM,
        scratch_shapes=[pltpu.SemaphoreType.DMA],
        compiler_params=PARAMS,
        name="pack_rest" if low else "pack_first",
    )(info, cache_keys, cache_values, swapped)


def spread_vertical(info, got, out):
    chip, core = info[0], info[1]
    mine = got[plane_row(vertical_block(info, member(chip)) >> 7), SLOTS2 - 2 :]
    for to in range(NV):
        out[to] = mine


def spread_call(info, got):
    return pl.pallas_call(
        spread_vertical,
        out_shape=jax.ShapeDtypeStruct((NV, 2, BLOCK, HD), jnp.bfloat16),
        in_specs=[SMEM, VMEM],
        out_specs=VMEM,
        compiler_params=PARAMS,
        name="spread_vertical",
    )(info, got)


def pack_second(info, *refs, rounds):
    got, out, sem = refs[:rounds], refs[rounds], refs[rounds + 1]
    chip, core = info[0], info[1]
    row_here = plane_row(chip)
    started = jnp.int32(0)
    for zh in range(4):
        block = (chip & 25) + zh * 2
        for j in range(NS):
            source = (STORED + block - offset(info, j)) >> 7
            lane = lane_of(info, j, block, source)
            frm = member(source)
            to = slot_of(info, j) * 2
            mine = plane_row(source) == row_here
            if rounds == 1:
                choices = [(mine, got[0], (zh * LANES + lane) * 2)]
            else:
                choices = [
                    (mine & (lane < LANES), got[0], (zh * LANES + lane) * 2),
                    (mine & (lane >= LANES), got[1], zh * 2),
                ]
            for test, ref, slot in choices:

                @pl.when(test)
                def _(ref=ref, slot=slot, frm=frm, zh=zh, to=to):
                    pltpu.make_async_copy(
                        ref.at[frm, pl.ds(slot, 2)], out.at[zh, pl.ds(to, 2)], sem
                    ).start()

            started = started + jnp.where(mine, 1, 0)
    source = vertical_block(info, member(chip)) >> 7
    mine = plane_row(source) == row_here
    for zh in range(4):

        @pl.when(mine)
        def _(zh=zh, frm=member(source)):
            pltpu.make_async_copy(
                got[0].at[frm, pl.ds(SLOTS - 2, 2)], out.at[zh, pl.ds(SLOTS2 - 2, 2)], sem
            ).start()

    started = started + jnp.where(mine, 4, 0)
    wait_for(sem, started, out.at[0, pl.ds(0, 2)])


def second_call(info, *got):
    def kernel(*refs):
        pack_second(*refs, rounds=len(got))

    return pl.pallas_call(
        kernel,
        out_shape=jax.ShapeDtypeStruct((4, SLOTS2, BLOCK, HD), jnp.bfloat16),
        in_specs=[SMEM] + [ANY] * len(got),
        out_specs=VMEM,
        scratch_shapes=[pltpu.SemaphoreType.DMA],
        compiler_params=PARAMS,
        name="pack_second",
    )(info, *got)


COLS = (NV + NS + 2) * BLOCK
CHUNK = 128


def attend(info, kept, swapped, got, vert, out, keys, values, theirs, sem):
    chip, core = info[0], info[1]
    copy = pltpu.make_async_copy(swapped.at[pl.ds(SWAP, (GROUP + 2) * OWN)], theirs, sem)
    copy.start()
    for v in range(NV):
        keys[v * BLOCK : (v + 1) * BLOCK] = vert[v, 0]
        values[v * BLOCK : (v + 1) * BLOCK] = vert[v, 1]
    column = lax.broadcasted_iota(jnp.int32, (1, COLS), 1)
    allowed = column < (NV + NS) * BLOCK
    for j in range(NS):
        block = STORED + chip - offset(info, j)
        frm = plane_row(block >> 7)
        at = (NV + j) * BLOCK
        slot = slot_of(info, j) * 2
        keys[at : at + BLOCK] = got[frm, slot]
        values[at : at + BLOCK] = got[frm, slot + 1]
        repeated = jnp.int32(0)
        for v in range(NV):
            repeated = repeated | jnp.where(vertical_block(info, v) == block, 1, 0)
        here = (column >= at) & (column < at + BLOCK)
        allowed = allowed & jnp.logical_not(here & (repeated == 1))
    copy.wait()
    low = core == 0
    at = (NV + NS) * BLOCK
    mine = pl.ds(pl.multiple_of(core * OWN, OWN) + at, OWN)
    rest = pl.ds(pl.multiple_of((1 - core) * OWN, OWN) + at, OWN)
    keys[mine] = kept[GROUP * OWN : (GROUP + 1) * OWN]
    values[mine] = kept[(GROUP + 1) * OWN :]
    keys[rest] = theirs[GROUP * OWN : (GROUP + 1) * OWN]
    values[rest] = theirs[(GROUP + 1) * OWN :]
    keys[at + BLOCK :] = jnp.zeros((BLOCK, HD), jnp.bfloat16)
    values[at + BLOCK :] = jnp.zeros((BLOCK, HD), jnp.bfloat16)
    row = lax.broadcasted_iota(jnp.int32, (CHUNK, COLS), 0) & (BLOCK - 1)
    col = lax.broadcasted_iota(jnp.int32, (CHUNK, COLS), 1)
    own = (col >= at) & (col - at <= row) & (col < at + BLOCK)
    keep = jnp.where(own, 1, 0) + jnp.where(allowed, 1, 0)
    scale = 1.0 / math.sqrt(HD)
    per = CHUNK // BLOCK
    for pair in range(GROUP // per):
        parts = []
        for i in range(per):
            g = pair * per + i
            some = slice(g * OWN, (g + 1) * OWN)
            parts += [
                jnp.where(low, kept[some], theirs[some]),
                jnp.where(low, theirs[some], kept[some]),
            ]
        q = jnp.concatenate(parts, axis=0)
        scores = lax.dot_general(
            q, keys[...], (((1,), (1,)), ((), ())), preferred_element_type=jnp.float32
        )
        scores = jnp.where(keep > 0, scores * scale, NEGATIVE)
        peak = jnp.max(scores, axis=-1, keepdims=True)
        weights = jnp.exp(scores - peak)
        total = jnp.sum(weights, axis=-1, keepdims=True)
        acc = jnp.dot(
            weights.astype(jnp.bfloat16), values[...], preferred_element_type=jnp.float32
        )
        result = (acc / total).astype(jnp.bfloat16)
        for i in range(per):
            cols = slice((pair * per + i) * HD, (pair * per + i + 1) * HD)
            for c in range(2):
                for y in range(4):
                    r = i * BLOCK + c * 32 + y * 8
                    out[y * 2 + c, :, cols] = result[r : r + 8]


def attend_call(info, kept, swapped, got, vert):
    return pl.pallas_call(
        attend,
        out_shape=jax.ShapeDtypeStruct((8, 8, GROUP * HD), jnp.bfloat16),
        in_specs=[SMEM, VMEM, ANY, VMEM, VMEM],
        out_specs=VMEM,
        scratch_shapes=[
            pltpu.VMEM((COLS, HD), jnp.bfloat16),
            pltpu.VMEM((COLS, HD), jnp.bfloat16),
            pltpu.VMEM(((GROUP + 2) * OWN, HD), jnp.bfloat16),
            pltpu.SemaphoreType.DMA,
        ],
        compiler_params=PARAMS,
        name="attend",
    )(info, kept, swapped, got, vert)


def too_many(slash):
    blocks = jnp.arange(32, dtype=jnp.int32)
    chips = (STORED + blocks[None, :] - slash[:, None]) >> 7
    same = jnp.sum((chips[:, None, :] == chips[None, :, :]).astype(jnp.int32), axis=1)
    return jnp.max(same) > LANES


def body(queries, cache_keys, cache_values, new_keys, new_values, vertical, slash):
    core = lax.axis_index("c").astype(jnp.int32)
    chip = (
        lax.axis_index("x") * 8 + lax.axis_index("zh") * 2 + lax.axis_index("zp")
    ).astype(jnp.int32)
    info = jnp.concatenate([jnp.stack([chip, core]), slash.reshape(-1), vertical.reshape(-1)])
    cache_keys, cache_values, queries, new_keys, new_values = (
        pltpu.with_memory_space_constraint(a, pltpu.HBM)
        for a in (cache_keys, cache_values, queries, new_keys, new_values)
    )
    own, kept = swap_call(info, cache_keys, cache_values, queries, new_keys, new_values)
    swapped = lax.ppermute(own, "c", [(0, 1), (1, 0)])
    cached = (cache_keys, cache_values, swapped)
    sent = first_call(info, *cached, 0, LANES)
    got = lax.all_to_all(sent, ("x", "zp"), 0, 0, tiled=True)

    def more():
        rest = first_call(info, *cached, LANES, 1)
        rest = lax.all_to_all(rest, ("x", "zp"), 0, 0, tiled=True)
        return second_call(info, got, rest)

    def enough():
        return second_call(info, got)

    sent = lax.cond(too_many(slash[core]), more, enough)
    got = lax.all_to_all(sent, "zh", 0, 0, tiled=True)
    vert = spread_call(info, got)
    vert = lax.all_to_all(vert, ("x", "zp"), 0, 0, tiled=True)
    out = attend_call(info, kept, swapped, got, vert)
    out = lax.all_to_all(out, ("y", "c"), 0, 0, tiled=True)
    return out.transpose(1, 0, 2).reshape(8, 8 * GROUP * HD)


def solution(mesh):
    parts = Mesh(mesh.devices.reshape(4, 4, 2, 2, 4), ("x", "zh", "zp", "c", "y"))
    ctx = ("x", "zh", "zp", "c")
    in_specs = (P(ctx, "y"),) * 5 + (P("y", None),) * 2
    out_specs = P(ctx + ("y",), None)
    return jax.shard_map(body, mesh=parts, in_specs=in_specs, out_specs=out_specs, check_vma=False)
```

```python
import math

import jax
import jax.numpy as jnp
from jax import lax
from jax.experimental import pallas as pl
from jax.experimental.pallas import tpu as pltpu
from jax.sharding import Mesh, PartitionSpec as P

HD = 128
BLOCK = 64
NV = 8
NS = 4
KVS = 2
GROUP = 8
STORED = 4096
PER_CHIP = 128
LANES = 3
NEGATIVE = -1e30
OWN = 32
SLOTS = (NS - 1) * 2
CHIP, CORE = NS + NV, NS + NV + 1
TRADED = NV * 2 * BLOCK
PAIRS = [(h, j) for h in range(KVS) for j in range(NS)]

SMEM = pl.BlockSpec(memory_space=pltpu.SMEM)
HBM = pl.BlockSpec(memory_space=pltpu.HBM)
ANY = pl.BlockSpec(memory_space=pl.ANY)
VMEM = pl.BlockSpec(memory_space=pltpu.VMEM)
PARAMS = pltpu.CompilerParams(vmem_limit_bytes=32 * 1024 * 1024)


def shaped(*shape):
    return jax.ShapeDtypeStruct(shape, jnp.bfloat16)


def window(info, h, j):
    return STORED - info[h, j]


def vertical_block(info, h, v):
    return info[h, NS + v]


def slot_of(info, h, j):
    slot = jnp.int32(0)
    for i in range(j):
        other = info[h, i]
        slot = slot + jnp.where((other == 32) | (other == STORED), 0, 1)
    mine = info[h, j]
    return jnp.where((mine == 32) | (mine == STORED), NS - 2, slot)


def member(chip):
    return (chip >> 3) * 2 + (chip & 1)


def plane_row(chip):
    return (chip >> 1) & 3


def wait_for(sem, count, like):
    def one(_, carry):
        pltpu.make_async_copy(like, like, sem).wait()
        return carry

    lax.fori_loop(0, count, one, 0)


def cached_block(core, h, block, mine, other, test, act):
    row = pl.multiple_of((block & 63) * BLOCK, BLOCK)
    at = (pl.ds(row, BLOCK), pl.ds(h * HD, HD))
    here = ((block >> 6) & 1) == core

    @pl.when(test & here)
    def _():
        act(mine[0].at[at], mine[1].at[at])

    @pl.when(test & jnp.logical_not(here))
    def _():
        act(other[0].at[at], other[1].at[at])


def pack_first(info, keys, values, other_keys, other_values, out, sem, *, low):
    chip, core = info[0, CHIP], info[0, CORE]
    spans = []
    for h, j in PAIRS:
        start = window(info, h, j)
        first = jnp.clip(chip * PER_CHIP - start, 0, 32)
        last = jnp.clip((chip + 1) * PER_CHIP - start, 0, 32)
        spans.append((start, first, last))
    started = jnp.int32(0)
    for i, (h, _) in enumerate(PAIRS):
        start, first, last = spans[i]

        def one(block, count, i=i, h=h, start=start):
            lane = jnp.int32(-low)
            for _, a, b in spans[:i]:
                lane = lane + jnp.where((block >= a) & (block < b), 1, 0)
            take = (lane >= 0) & (lane < LANES)
            slot = (plane_row(block) * LANES + lane) * 2
            to = member(block)

            def act(key_rows, value_rows):
                pltpu.make_async_copy(key_rows, out.at[to, slot], sem).start()
                pltpu.make_async_copy(value_rows, out.at[to, slot + 1], sem).start()

            cached_block(
                core, h, start + block, (keys, values), (other_keys, other_values), take, act
            )
            return count + jnp.where(take, 2, 0)

        started = lax.fori_loop(first, last, one, started)
    wait_for(sem, started, out.at[0, 0])


def first_call(info, cached, low):
    def kernel(*refs):
        pack_first(*refs, low=low)

    return pl.pallas_call(
        kernel,
        out_shape=shaped(8, 4 * LANES * 2, BLOCK, HD),
        in_specs=[SMEM] + [HBM] * 4,
        out_specs=VMEM,
        scratch_shapes=[pltpu.SemaphoreType.DMA],
        compiler_params=PARAMS,
        name="pack_rest" if low else "pack_first",
    )(info, *cached)


def pack_second(info, *refs, rounds):
    got, out, sem = refs[:rounds], refs[rounds], refs[rounds + 1]
    chip = info[0, CHIP]
    row_here = plane_row(chip)
    started = jnp.int32(0)
    for zh in range(4):
        block = (chip & 25) + zh * 2
        sources = [(window(info, h, j) + block) >> 7 for h, j in PAIRS]
        for i, (h, j) in enumerate(PAIRS):
            source = sources[i]
            lane = jnp.int32(0)
            for before in sources[:i]:
                lane = lane + jnp.where(before == source, 1, 0)
            frm = member(source)
            to = h * SLOTS + slot_of(info, h, j) * 2
            mine = plane_row(source) == row_here
            for r, ref in enumerate(got):
                test, slot = mine, (zh * LANES + lane - r * LANES) * 2
                if rounds > 1:
                    test = mine & (lane >= r * LANES) & (lane < (r + 1) * LANES)

                @pl.when(test)
                def _(ref=ref, slot=slot, frm=frm, zh=zh, to=to):
                    pltpu.make_async_copy(
                        ref.at[frm, pl.ds(slot, 2)], out.at[zh, pl.ds(to, 2)], sem
                    ).start()

            started = started + jnp.where(mine, 1, 0)
    wait_for(sem, started, out.at[0, pl.ds(0, 2)])


def second_call(info, *got):
    def kernel(*refs):
        pack_second(*refs, rounds=len(got))

    return pl.pallas_call(
        kernel,
        out_shape=shaped(4, KVS * SLOTS, BLOCK, HD),
        in_specs=[SMEM] + [ANY] * len(got),
        out_specs=VMEM,
        scratch_shapes=[pltpu.SemaphoreType.DMA],
        compiler_params=PARAMS,
        name="pack_second",
    )(info, *got)


def pack_queries(core, queries, new_keys, new_values, send):
    other = 1 - core
    for g in range(GROUP):
        at = TRADED + g * OWN
        send[at : at + OWN] = queries[:, (other * GROUP + g) * HD : (other * GROUP + g + 1) * HD]
    at = TRADED + GROUP * OWN
    send[at : at + OWN] = new_keys[:, other * HD : (other + 1) * HD]
    send[at + OWN : at + 2 * OWN] = new_values[:, other * HD : (other + 1) * HD]


def finish_slash(info, got, queries, new_keys, new_values, keep, send):
    chip = info[0, CHIP]
    for h, j in PAIRS:
        frm = plane_row((window(info, h, j) + chip) >> 7)
        slot = h * SLOTS + slot_of(info, h, j) * 2
        if h == 0:
            keep[j] = got[frm, pl.ds(slot, 2)]
        else:
            send[j * 2 * BLOCK : (j * 2 + 1) * BLOCK] = got[frm, slot]
            send[(j * 2 + 1) * BLOCK : (j + 1) * 2 * BLOCK] = got[frm, slot + 1]
    pack_queries(0, queries, new_keys, new_values, send)


def finish_vertical(info, got, queries, new_keys, new_values, keep, send):
    for v in range(NV):
        keep[v] = got[v, 2:]
        send[v * 2 * BLOCK : (v * 2 + 1) * BLOCK] = got[v, 0]
        send[(v * 2 + 1) * BLOCK : (v + 1) * 2 * BLOCK] = got[v, 1]
    pack_queries(1, queries, new_keys, new_values, send)


def finish_call(kernel, info, got, rows):
    return pl.pallas_call(
        kernel,
        out_shape=(shaped(NV, 2, BLOCK, HD), shaped(TRADED + (GROUP + 2) * OWN, HD)),
        in_specs=[SMEM] + [VMEM] * 4,
        out_specs=(VMEM, VMEM),
        compiler_params=PARAMS,
        name=kernel.__name__,
    )(info, got, *rows)


def pack_vertical(info, keys, values, other_keys, other_values, out, sem):
    chip, core = info[0, CHIP], info[0, CORE]
    started = jnp.int32(0)
    for h in range(KVS):
        for v in range(NV):
            block = vertical_block(info, h, v)
            mine = (block >> 7) == chip

            def act(key_rows, value_rows, h=h, v=v):
                pltpu.make_async_copy(key_rows, out.at[v, 2 * h], sem).start()
                pltpu.make_async_copy(value_rows, out.at[v, 2 * h + 1], sem).start()

            cached_block(core, h, block, (keys, values), (other_keys, other_values), mine, act)
            started = started + jnp.where(mine, 2, 0)
    wait_for(sem, started, out.at[0, 0])


def pack_vertical_call(info, cached):
    return pl.pallas_call(
        pack_vertical,
        out_shape=shaped(NV, 2 * KVS, BLOCK, HD),
        in_specs=[SMEM] + [HBM] * 4,
        out_specs=VMEM,
        scratch_shapes=[pltpu.SemaphoreType.DMA],
        compiler_params=PARAMS,
        name="pack_vertical",
    )(info, *cached)


def spread_rows(info, got, out):
    here = member(info[0, CHIP])
    for h in range(KVS):
        mine = got[member(vertical_block(info, h, here) >> 7), 2 * h : 2 * h + 2]
        for to in range(4):
            out[to, 2 * h : 2 * h + 2] = mine


def spread_members(info, got, out):
    here = member(info[0, CHIP])
    for h in range(KVS):
        mine = got[plane_row(vertical_block(info, h, here) >> 7), 2 * h : 2 * h + 2]
        for to in range(NV):
            out[to, 2 * h : 2 * h + 2] = mine


def spread_call(kernel, copies, info, got):
    return pl.pallas_call(
        kernel,
        out_shape=shaped(copies, 2 * KVS, BLOCK, HD),
        in_specs=[SMEM, VMEM],
        out_specs=VMEM,
        compiler_params=PARAMS,
        name=kernel.__name__,
    )(info, got)


COLS = (NV + NS + 2) * BLOCK
CHUNK = 128


def attend(info, queries, new_keys, new_values, keep, theirs, out, keys, values, rows):
    chip, core = info[0, CHIP], info[0, CORE]
    ours = core == 0
    verticals, slashes = 0, NV * BLOCK

    @pl.when(ours)
    def _():
        for j in range(NS):
            at = slashes + j * BLOCK
            keys[at : at + BLOCK] = keep[j, 0]
            values[at : at + BLOCK] = keep[j, 1]
        for v in range(NV):
            at = verticals + v * BLOCK
            keys[at : at + BLOCK] = theirs[v * 2 * BLOCK : (v * 2 + 1) * BLOCK]
            values[at : at + BLOCK] = theirs[(v * 2 + 1) * BLOCK : (v + 1) * 2 * BLOCK]

    @pl.when(jnp.logical_not(ours))
    def _():
        for j in range(NS):
            at = slashes + j * BLOCK
            keys[at : at + BLOCK] = theirs[j * 2 * BLOCK : (j * 2 + 1) * BLOCK]
            values[at : at + BLOCK] = theirs[(j * 2 + 1) * BLOCK : (j + 1) * 2 * BLOCK]
        for v in range(NV):
            at = verticals + v * BLOCK
            keys[at : at + BLOCK] = keep[v, 0]
            values[at : at + BLOCK] = keep[v, 1]

    column = lax.broadcasted_iota(jnp.int32, (1, COLS), 1)
    allowed = column < (NV + NS) * BLOCK
    for j in range(NS):
        block = window(info, core, j) + chip
        at = slashes + j * BLOCK
        repeated = jnp.int32(0)
        for v in range(NV):
            repeated = repeated | jnp.where(vertical_block(info, core, v) == block, 1, 0)
        here = (column >= at) & (column < at + BLOCK)
        allowed = allowed & jnp.logical_not(here & (repeated == 1))
    mine = pl.multiple_of(core * OWN, OWN)
    rest = pl.multiple_of((1 - core) * OWN, OWN)
    for g in range(GROUP):
        cols = pl.ds(pl.multiple_of((core * GROUP + g) * HD, HD), HD)
        rows[pl.ds(mine + g * BLOCK, OWN)] = queries[:, cols]
        at = TRADED + g * OWN
        rows[pl.ds(rest + g * BLOCK, OWN)] = theirs[at : at + OWN]
    at = (NV + NS) * BLOCK
    cols = pl.ds(pl.multiple_of(core * HD, HD), HD)
    fresh = TRADED + GROUP * OWN
    keys[pl.ds(mine + at, OWN)] = new_keys[:, cols]
    values[pl.ds(mine + at, OWN)] = new_values[:, cols]
    keys[pl.ds(rest + at, OWN)] = theirs[fresh : fresh + OWN]
    values[pl.ds(rest + at, OWN)] = theirs[fresh + OWN : fresh + 2 * OWN]
    keys[at + BLOCK :] = jnp.zeros((BLOCK, HD), jnp.bfloat16)
    values[at + BLOCK :] = jnp.zeros((BLOCK, HD), jnp.bfloat16)
    row = lax.broadcasted_iota(jnp.int32, (CHUNK, COLS), 0) & (BLOCK - 1)
    col = lax.broadcasted_iota(jnp.int32, (CHUNK, COLS), 1)
    own = (col >= at) & (col - at <= row) & (col < at + BLOCK)
    kept = jnp.where(own, 1, 0) + jnp.where(allowed, 1, 0)
    scale = 1.0 / math.sqrt(HD)
    per = CHUNK // BLOCK
    for pair in range(GROUP // per):
        scores = lax.dot_general(
            rows[pair * CHUNK : (pair + 1) * CHUNK],
            keys[...],
            (((1,), (1,)), ((), ())),
            preferred_element_type=jnp.float32,
        )
        scores = jnp.where(kept > 0, scores * scale, NEGATIVE)
        peak = jnp.max(scores, axis=-1, keepdims=True)
        weights = jnp.exp(scores - peak)
        total = jnp.sum(weights, axis=-1, keepdims=True)
        acc = jnp.dot(
            weights.astype(jnp.bfloat16), values[...], preferred_element_type=jnp.float32
        )
        result = (acc / total).astype(jnp.bfloat16)
        for i in range(per):
            cols = slice((pair * per + i) * HD, (pair * per + i + 1) * HD)
            for c in range(2):
                for y in range(4):
                    r = i * BLOCK + c * 32 + y * 8
                    out[y * 2 + c, :, cols] = result[r : r + 8]


def attend_call(info, rows, keep, theirs):
    return pl.pallas_call(
        attend,
        out_shape=shaped(8, 8, GROUP * HD),
        in_specs=[SMEM] + [VMEM] * 5,
        out_specs=VMEM,
        scratch_shapes=[
            pltpu.VMEM((COLS, HD), jnp.bfloat16),
            pltpu.VMEM((COLS, HD), jnp.bfloat16),
            pltpu.VMEM((GROUP * BLOCK, HD), jnp.bfloat16),
        ],
        compiler_params=PARAMS,
        name="attend",
    )(info, *rows, keep, theirs)


def too_many(slash):
    blocks = jnp.arange(32, dtype=jnp.int32)
    chips = ((STORED + blocks[None, None, :] - slash[:, :, None]) >> 7).reshape(KVS * NS, 32)
    same = jnp.sum((chips[:, None, :] == chips[None, :, :]).astype(jnp.int32), axis=1)
    return jnp.max(same) > LANES


def exchange(blocks, axes):
    return lax.all_to_all(blocks, axes, 0, 0, tiled=True)


def body(queries, cache_keys, cache_values, new_keys, new_values, vertical, slash):
    core = lax.axis_index("c").astype(jnp.int32)
    chip = (
        lax.axis_index("x") * 8 + lax.axis_index("zh") * 2 + lax.axis_index("zp")
    ).astype(jnp.int32)
    here = jnp.broadcast_to(jnp.stack([chip, core]), (2, 2))
    info = jnp.concatenate([slash, vertical, here], axis=1)
    rows = (queries, new_keys, new_values)
    swap = [(0, 1), (1, 0)]
    cached = (
        cache_keys,
        cache_values,
        lax.ppermute(cache_keys, "c", swap),
        lax.ppermute(cache_values, "c", swap),
    )
    cached = tuple(pltpu.with_memory_space_constraint(a, pltpu.HBM) for a in cached)
    again = too_many(slash)

    def slashes():
        got = exchange(first_call(info, cached, 0), ("x", "zp"))

        def more():
            rest = exchange(first_call(info, cached, LANES), ("x", "zp"))
            return second_call(info, got, rest)

        sent = lax.cond(again, more, lambda: second_call(info, got))
        return finish_call(finish_slash, info, exchange(sent, "zh"), rows)

    def verticals():
        got = exchange(pack_vertical_call(info, cached), ("x", "zp"))
        got = exchange(spread_call(spread_rows, 4, info, got), "zh")
        got = exchange(spread_call(spread_members, NV, info, got), ("x", "zp"))
        return finish_call(finish_vertical, info, got, rows)

    keep, send = lax.cond(core == 0, slashes, verticals)
    theirs = lax.ppermute(send, "c", swap)
    out = attend_call(info, rows, keep, theirs)
    out = lax.all_to_all(out, ("y", "c"), 0, 0, tiled=True)
    return out.transpose(1, 0, 2).reshape(8, 8 * GROUP * HD)


def solution(mesh):
    parts = Mesh(mesh.devices.reshape(4, 4, 2, 2, 4), ("x", "zh", "zp", "c", "y"))
    ctx = ("x", "zh", "zp", "c")
    in_specs = (P(ctx, "y"),) * 5 + (P("y", None),) * 2
    out_specs = P(ctx + ("y",), None)
    return jax.shard_map(body, mesh=parts, in_specs=in_specs, out_specs=out_specs, check_vma=False)
```

```python
import math

import jax
import jax.numpy as jnp
from jax import lax
from jax.experimental import pallas as pl
from jax.experimental.pallas import tpu as pltpu
from jax.sharding import Mesh, PartitionSpec as P

HD = 128
BLOCK = 64
NV = 8
NS = 4
KVS = 2
GROUP = 8
STORED = 4096
PER_CHIP = 128
LANES = 3
NEGATIVE = -1e30
OWN = 32
SLOTS = (NS - 1) * 2
FREE = 2
CHIP, CORE = FREE + NV, FREE + NV + 1
ENDS = (0, PER_CHIP // 4 - 1)
TRADED = NV * 2 * BLOCK
PAIRS = [(h, j) for h in range(KVS) for j in range(FREE)]

SMEM = pl.BlockSpec(memory_space=pltpu.SMEM)
HBM = pl.BlockSpec(memory_space=pltpu.HBM)
ANY = pl.BlockSpec(memory_space=pl.ANY)
VMEM = pl.BlockSpec(memory_space=pltpu.VMEM)
PARAMS = pltpu.CompilerParams(vmem_limit_bytes=32 * 1024 * 1024)


def shaped(*shape):
    return jax.ShapeDtypeStruct(shape, jnp.bfloat16)


def window(info, h, j):
    return STORED - info[h, j]


def vertical_block(info, h, v):
    return info[h, FREE + v]


def member(chip):
    return (chip >> 3) * 2 + (chip & 1)


def plane_row(chip):
    return (chip >> 1) & 3


def wait_for(sem, count, like):
    def one(_, carry):
        pltpu.make_async_copy(like, like, sem).wait()
        return carry

    lax.fori_loop(0, count, one, 0)


def cached_block(core, h, block, mine, other, test, act):
    at = ((block >> 1) & 31, block & 1, slice(None), pl.ds(h * HD, HD))
    here = ((block >> 6) & 1) == core

    @pl.when(test & here)
    def _():
        act(mine[0].at[at], mine[1].at[at])

    @pl.when(test & jnp.logical_not(here))
    def _():
        act(other[0].at[at], other[1].at[at])


def pack_first(info, keys, values, other_keys, other_values, out, sem, *, low):
    chip, core = info[0, CHIP], info[0, CORE]
    if not low:
        for end, pair, caches in (
            (ENDS[0], 0, (keys, values)),
            (ENDS[1], 16, (other_keys, other_values)),
        ):

            @pl.when(chip == end)
            def _(pair=pair, caches=caches):
                copies = []
                for to in range(8):
                    pairs = pl.ds(pair + (to >> 1) * 4, 4)
                    for h in range(KVS):
                        for k, cache in enumerate(caches):
                            copies.append(
                                pltpu.make_async_copy(
                                    cache.at[pairs, to & 1, :, pl.ds(h * HD, HD)],
                                    out.at[to, :, 2 * h + k],
                                    sem,
                                )
                            )
                for c in copies:
                    c.start()
                for c in copies:
                    c.wait()

    base = jnp.where((chip == ENDS[0]) | (chip == ENDS[1]), KVS, 0) - low
    spans = []
    for h, j in PAIRS:
        start = window(info, h, j)
        first = jnp.clip(chip * PER_CHIP - start, 0, 32)
        last = jnp.clip((chip + 1) * PER_CHIP - start, 0, 32)
        spans.append((start, first, last))
    started = jnp.int32(0)
    for i, (h, _) in enumerate(PAIRS):
        start, first, last = spans[i]

        def one(block, count, i=i, h=h, start=start):
            lane = base
            for _, a, b in spans[:i]:
                lane = lane + jnp.where((block >= a) & (block < b), 1, 0)
            take = (lane >= 0) & (lane < LANES)
            row, to = plane_row(block), member(block)

            def act(key_rows, value_rows):
                pltpu.make_async_copy(key_rows, out.at[to, row, lane * 2], sem).start()
                pltpu.make_async_copy(value_rows, out.at[to, row, lane * 2 + 1], sem).start()

            cached_block(
                core, h, start + block, (keys, values), (other_keys, other_values), take, act
            )
            return count + jnp.where(take, 2, 0)

        started = lax.fori_loop(first, last, one, started)
    wait_for(sem, started, out.at[0, 0, 0])


def first_call(info, cached, low):
    def kernel(*refs):
        pack_first(*refs, low=low)

    return pl.pallas_call(
        kernel,
        out_shape=shaped(8, 4, LANES * 2, BLOCK, HD),
        in_specs=[SMEM, HBM, HBM, ANY, ANY],
        out_specs=VMEM,
        scratch_shapes=[pltpu.SemaphoreType.DMA],
        compiler_params=PARAMS,
        name="pack_rest" if low else "pack_first",
    )(info, *cached)


def pack_second(info, *refs, rounds):
    got, out = refs[:rounds], refs[rounds]
    chip = info[0, CHIP]
    row_here = plane_row(chip)
    for end in ENDS:

        @pl.when(row_here == plane_row(end))
        def _(end=end):
            for zh in range(4):
                for h in range(KVS):
                    at = h * SLOTS + FREE * 2
                    out[zh, at : at + 2] = got[0][member(end), zh, 2 * h : 2 * h + 2]

    for zh in range(4):
        block = (chip & 25) + zh * 2
        sources = [(window(info, h, j) + block) >> 7 for h, j in PAIRS]
        for i, (h, j) in enumerate(PAIRS):

            @pl.when(plane_row(sources[i]) == row_here)
            def _(zh=zh, i=i, at=h * SLOTS + j * 2, sources=sources):
                source = sources[i]
                lane = jnp.where((source == ENDS[0]) | (source == ENDS[1]), KVS, 0)
                for before in sources[:i]:
                    lane = lane + jnp.where(before == source, 1, 0)
                for r, ref in enumerate(got):

                    def copy(ref=ref, lane=lane - r * LANES):
                        out[zh, at : at + 2] = ref[member(source), zh, pl.ds(lane * 2, 2)]

                    if rounds == 1:
                        copy()
                    else:
                        pl.when((lane >= r * LANES) & (lane < (r + 1) * LANES))(copy)


def second_call(info, *got):
    def kernel(*refs):
        pack_second(*refs, rounds=len(got))

    return pl.pallas_call(
        kernel,
        out_shape=shaped(4, KVS * SLOTS, BLOCK, HD),
        in_specs=[SMEM] + [VMEM] * len(got),
        out_specs=VMEM,
        compiler_params=PARAMS,
        name="pack_second",
    )(info, *got)


def pack_queries(core, queries, new_keys, new_values, send):
    other = 1 - core
    for g in range(GROUP):
        at = TRADED + g * OWN
        send[at : at + OWN] = queries[:, (other * GROUP + g) * HD : (other * GROUP + g + 1) * HD]
    at = TRADED + GROUP * OWN
    send[at : at + OWN] = new_keys[:, other * HD : (other + 1) * HD]
    send[at + OWN : at + 2 * OWN] = new_values[:, other * HD : (other + 1) * HD]


def finish_slash(info, got, queries, new_keys, new_values, keep, send):
    chip = info[0, CHIP]
    for h in range(KVS):
        for j in range(NS):
            if j < FREE:
                frm, slot = plane_row((window(info, h, j) + chip) >> 7), h * SLOTS + j * 2
            else:
                frm, slot = plane_row(ENDS[j - FREE]), h * SLOTS + FREE * 2
            if h == 0:
                keep[j] = got[frm, slot : slot + 2]
            else:
                send[j * 2 * BLOCK : (j * 2 + 1) * BLOCK] = got[frm, slot]
                send[(j * 2 + 1) * BLOCK : (j + 1) * 2 * BLOCK] = got[frm, slot + 1]
    pack_queries(0, queries, new_keys, new_values, send)


def finish_vertical(info, got, queries, new_keys, new_values, keep, send):
    for v in range(NV):
        keep[v] = got[v, 2:]
        send[v * 2 * BLOCK : (v * 2 + 1) * BLOCK] = got[v, 0]
        send[(v * 2 + 1) * BLOCK : (v + 1) * 2 * BLOCK] = got[v, 1]
    pack_queries(1, queries, new_keys, new_values, send)


def finish_call(kernel, info, got, rows):
    return pl.pallas_call(
        kernel,
        out_shape=(shaped(NV, 2, BLOCK, HD), shaped(TRADED + (GROUP + 2) * OWN, HD)),
        in_specs=[SMEM] + [VMEM] * 4,
        out_specs=(VMEM, VMEM),
        compiler_params=PARAMS,
        name=kernel.__name__,
    )(info, got, *rows)


def pack_vertical(info, keys, values, other_keys, other_values, out, sem):
    chip, core = info[0, CHIP], info[0, CORE]
    started = jnp.int32(0)
    for h in range(KVS):
        for v in range(NV):
            block = vertical_block(info, h, v)
            mine = (block >> 7) == chip

            def act(key_rows, value_rows, h=h, v=v):
                pltpu.make_async_copy(key_rows, out.at[v, 2 * h], sem).start()
                pltpu.make_async_copy(value_rows, out.at[v, 2 * h + 1], sem).start()

            cached_block(core, h, block, (keys, values), (other_keys, other_values), mine, act)
            started = started + jnp.where(mine, 2, 0)
    wait_for(sem, started, out.at[0, 0])


def pack_vertical_call(info, cached):
    return pl.pallas_call(
        pack_vertical,
        out_shape=shaped(NV, 2 * KVS, BLOCK, HD),
        in_specs=[SMEM, HBM, HBM, ANY, ANY],
        out_specs=VMEM,
        scratch_shapes=[pltpu.SemaphoreType.DMA],
        compiler_params=PARAMS,
        name="pack_vertical",
    )(info, *cached)


def spread_rows(info, got, out):
    here = member(info[0, CHIP])
    for h in range(KVS):
        mine = got[member(vertical_block(info, h, here) >> 7), 2 * h : 2 * h + 2]
        for to in range(4):
            out[to, 2 * h : 2 * h + 2] = mine


def spread_members(info, got, out):
    here = member(info[0, CHIP])
    for h in range(KVS):
        mine = got[plane_row(vertical_block(info, h, here) >> 7), 2 * h : 2 * h + 2]
        for to in range(NV):
            out[to, 2 * h : 2 * h + 2] = mine


def spread_call(kernel, copies, info, got):
    return pl.pallas_call(
        kernel,
        out_shape=shaped(copies, 2 * KVS, BLOCK, HD),
        in_specs=[SMEM, VMEM],
        out_specs=VMEM,
        compiler_params=PARAMS,
        name=kernel.__name__,
    )(info, got)


COLS = (NV + NS + 2) * BLOCK
CHUNK = 256


def attend(info, queries, new_keys, new_values, keep, theirs, out, keys, values, rows):
    chip, core = info[0, CHIP], info[0, CORE]
    ours = core == 0
    verticals, slashes = 0, NV * BLOCK

    @pl.when(ours)
    def _():
        for j in range(NS):
            at = slashes + j * BLOCK
            keys[at : at + BLOCK] = keep[j, 0]
            values[at : at + BLOCK] = keep[j, 1]
        for v in range(NV):
            at = verticals + v * BLOCK
            keys[at : at + BLOCK] = theirs[v * 2 * BLOCK : (v * 2 + 1) * BLOCK]
            values[at : at + BLOCK] = theirs[(v * 2 + 1) * BLOCK : (v + 1) * 2 * BLOCK]

    @pl.when(jnp.logical_not(ours))
    def _():
        for j in range(NS):
            at = slashes + j * BLOCK
            keys[at : at + BLOCK] = theirs[j * 2 * BLOCK : (j * 2 + 1) * BLOCK]
            values[at : at + BLOCK] = theirs[(j * 2 + 1) * BLOCK : (j + 1) * 2 * BLOCK]
        for v in range(NV):
            at = verticals + v * BLOCK
            keys[at : at + BLOCK] = keep[v, 0]
            values[at : at + BLOCK] = keep[v, 1]

    column = lax.broadcasted_iota(jnp.int32, (1, COLS), 1)
    allowed = column < (NV + NS) * BLOCK
    for j in range(NS):
        start = window(info, core, j) if j < FREE else (0, STORED - 32)[j - FREE]
        block = start + chip
        at = slashes + j * BLOCK
        repeated = jnp.int32(0)
        for v in range(NV):
            repeated = repeated | jnp.where(vertical_block(info, core, v) == block, 1, 0)
        here = (column >= at) & (column < at + BLOCK)
        allowed = allowed & jnp.logical_not(here & (repeated == 1))
    mine = pl.multiple_of(core * OWN, OWN)
    rest = pl.multiple_of((1 - core) * OWN, OWN)
    for g in range(GROUP):
        cols = pl.ds(pl.multiple_of((core * GROUP + g) * HD, HD), HD)
        rows[pl.ds(mine + g * BLOCK, OWN)] = queries[:, cols]
        at = TRADED + g * OWN
        rows[pl.ds(rest + g * BLOCK, OWN)] = theirs[at : at + OWN]
    at = (NV + NS) * BLOCK
    cols = pl.ds(pl.multiple_of(core * HD, HD), HD)
    fresh = TRADED + GROUP * OWN
    keys[pl.ds(mine + at, OWN)] = new_keys[:, cols]
    values[pl.ds(mine + at, OWN)] = new_values[:, cols]
    keys[pl.ds(rest + at, OWN)] = theirs[fresh : fresh + OWN]
    values[pl.ds(rest + at, OWN)] = theirs[fresh + OWN : fresh + 2 * OWN]
    keys[at + BLOCK :] = jnp.zeros((BLOCK, HD), jnp.bfloat16)
    values[at + BLOCK :] = jnp.zeros((BLOCK, HD), jnp.bfloat16)
    row = lax.broadcasted_iota(jnp.int32, (CHUNK, COLS), 0) & (BLOCK - 1)
    col = lax.broadcasted_iota(jnp.int32, (CHUNK, COLS), 1)
    own = (col >= at) & (col - at <= row) & (col < at + BLOCK)
    kept = own | allowed
    scale = math.log2(math.e) / math.sqrt(HD)
    per = CHUNK // BLOCK
    for pair in range(GROUP // per):
        scores = lax.dot_general(
            rows[pair * CHUNK : (pair + 1) * CHUNK],
            keys[...],
            (((1,), (1,)), ((), ())),
            preferred_element_type=jnp.float32,
        )
        scores = jnp.where(kept, scores, NEGATIVE)
        peak = jnp.max(scores, axis=-1, keepdims=True)
        weights = jnp.exp2((scores - peak) * scale)
        total = jnp.sum(weights, axis=-1, keepdims=True)
        acc = jnp.dot(
            weights.astype(jnp.bfloat16), values[...], preferred_element_type=jnp.float32
        )
        result = (acc / total).astype(jnp.bfloat16)
        for i in range(per):
            cols = slice((pair * per + i) * HD, (pair * per + i + 1) * HD)
            for c in range(2):
                for y in range(4):
                    r = i * BLOCK + c * 32 + y * 8
                    out[y * 2 + c, :, cols] = result[r : r + 8]


def attend_call(info, rows, keep, theirs):
    return pl.pallas_call(
        attend,
        out_shape=shaped(8, 8, GROUP * HD),
        in_specs=[SMEM] + [VMEM] * 5,
        out_specs=VMEM,
        scratch_shapes=[
            pltpu.VMEM((COLS, HD), jnp.bfloat16),
            pltpu.VMEM((COLS, HD), jnp.bfloat16),
            pltpu.VMEM((GROUP * BLOCK, HD), jnp.bfloat16),
        ],
        compiler_params=PARAMS,
        name="attend",
    )(info, *rows, keep, theirs)


def too_many(slash):
    blocks = jnp.arange(32, dtype=jnp.int32)
    chips = ((STORED + blocks[None, None, :] - slash[:, :, None]) >> 7).reshape(KVS * NS, 32)
    same = jnp.sum((chips[:, None, :] == chips[None, :, :]).astype(jnp.int32), axis=1)
    return jnp.max(same) > LANES


def exchange(blocks, axes):
    return lax.all_to_all(blocks, axes, 0, 0, tiled=True)


def body(queries, cache_keys, cache_values, new_keys, new_values, vertical, slash):
    core = lax.axis_index("c").astype(jnp.int32)
    chip = (
        lax.axis_index("x") * 8 + lax.axis_index("zh") * 2 + lax.axis_index("zp")
    ).astype(jnp.int32)
    again = too_many(slash)
    here = jnp.broadcast_to(jnp.stack([chip, core, again.astype(jnp.int32)]), (2, 3))
    fixed = (slash == 32) | (slash == STORED)
    free = jnp.stack(
        [
            jnp.min(jnp.where(fixed, STORED, slash), axis=1),
            jnp.max(jnp.where(fixed, 32, slash), axis=1),
        ],
        axis=1,
    )
    info = jnp.concatenate([free, vertical, here], axis=1)
    rows = (queries, new_keys, new_values)
    swap = [(0, 1), (1, 0)]
    cached = (
        cache_keys,
        cache_values,
        lax.ppermute(cache_keys, "c", swap),
        lax.ppermute(cache_values, "c", swap),
    )
    cached = tuple(a.reshape(32, 2, BLOCK, KVS * HD) for a in cached)
    cached = tuple(pltpu.with_memory_space_constraint(a, pltpu.HBM) for a in cached[:2]) + cached[2:]

    def slashes():
        got = exchange(first_call(info, cached, 0), ("x", "zp"))

        def more():
            rest = exchange(first_call(info, cached, LANES), ("x", "zp"))
            return second_call(info, got, rest)

        sent = lax.cond(again, more, lambda: second_call(info, got))
        return finish_call(finish_slash, info, exchange(sent, "zh"), rows)

    def verticals():
        got = exchange(pack_vertical_call(info, cached), ("x", "zp"))
        got = exchange(spread_call(spread_rows, 4, info, got), "zh")
        got = exchange(spread_call(spread_members, NV, info, got), ("x", "zp"))
        return finish_call(finish_vertical, info, got, rows)

    keep, send = lax.cond(core == 0, slashes, verticals)
    theirs = lax.ppermute(send, "c", swap)
    out = attend_call(info, rows, keep, theirs)
    out = lax.all_to_all(out, ("y", "c"), 0, 0, tiled=True)
    return out.transpose(1, 0, 2).reshape(8, 8 * GROUP * HD)


def solution(mesh):
    parts = Mesh(mesh.devices.reshape(4, 4, 2, 2, 4), ("x", "zh", "zp", "c", "y"))
    ctx = ("x", "zh", "zp", "c")
    in_specs = (P(ctx, "y"),) * 5 + (P("y", None),) * 2
    out_specs = P(ctx + ("y",), None)
    return jax.shard_map(body, mesh=parts, in_specs=in_specs, out_specs=out_specs, check_vma=False)
```

```python
import functools
import math

import jax
import jax.numpy as jnp
from jax import lax
from jax.experimental import pallas as pl
from jax.experimental.pallas import tpu as pltpu
from jax.sharding import Mesh, PartitionSpec as P

HD = 128
BLOCK = 64
NV = 8
NS = 4
KVS = 2
GROUP = 8
STORED = 4096
PER_CHIP = 128
LANES = (2, 3, 4, 6)
NEGATIVE = -1e30
OWN = 32
SLOTS = (NS - 1) * 2
FREE = 2
CHIP, CORE = FREE + NV, FREE + NV + 1
ENDS = (0, PER_CHIP // 4 - 1)
TRADED = NV * 2 * BLOCK
PAIRS = [(h, j) for h in range(KVS) for j in range(FREE)]

SMEM = pl.BlockSpec(memory_space=pltpu.SMEM)
HBM = pl.BlockSpec(memory_space=pltpu.HBM)
ANY = pl.BlockSpec(memory_space=pl.ANY)
VMEM = pl.BlockSpec(memory_space=pltpu.VMEM)
PARAMS = pltpu.CompilerParams(vmem_limit_bytes=32 * 1024 * 1024)


def shaped(*shape):
    return jax.ShapeDtypeStruct(shape, jnp.bfloat16)


def window(info, h, j):
    return STORED - info[h, j]


def vertical_block(info, h, v):
    return info[h, FREE + v]


def member(chip):
    return (chip >> 3) * 2 + (chip & 1)


def plane_row(chip):
    return (chip >> 1) & 3


def wait_for(sem, count, like):
    def one(_, carry):
        pltpu.make_async_copy(like, like, sem).wait()
        return carry

    lax.fori_loop(0, count, one, 0)


def cached_block(core, h, block, mine, other, test, act):
    at = ((block >> 1) & 31, block & 1, slice(None), pl.ds(h * HD, HD))
    here = ((block >> 6) & 1) == core

    @pl.when(here & test)
    def _():
        act(mine[0].at[at], mine[1].at[at])

    @pl.when(jnp.logical_not(here) & test)
    def _():
        act(other[0].at[at], other[1].at[at])


def pack_first(info, keys, values, other_keys, other_values, out, sem):
    chip, core = info[0, CHIP], info[0, CORE]
    for end, pair, caches in (
        (ENDS[0], 0, (keys, values)),
        (ENDS[1], 16, (other_keys, other_values)),
    ):

        @pl.when(chip == end)
        def _(pair=pair, caches=caches):
            copies = []
            for to in range(8):
                pairs = pl.ds(pair + (to >> 1) * 4, 4)
                for h in range(KVS):
                    for k, cache in enumerate(caches):
                        copies.append(
                            pltpu.make_async_copy(
                                cache.at[pairs, to & 1, :, pl.ds(h * HD, HD)],
                                out.at[to, :, 2 * h + k],
                                sem,
                            )
                        )
            for c in copies:
                c.start()
            for c in copies:
                c.wait()

    base = jnp.where((chip == ENDS[0]) | (chip == ENDS[1]), KVS, 0)
    spans = []
    for h, j in PAIRS:
        start = window(info, h, j)
        first = jnp.clip(chip * PER_CHIP - start, 0, 32)
        last = jnp.clip((chip + 1) * PER_CHIP - start, 0, 32)
        spans.append((start, first, last))
    started = jnp.int32(0)
    for i, (h, _) in enumerate(PAIRS):
        start, first, last = spans[i]

        def one(block, count, i=i, h=h, start=start):
            lane = base
            for _, a, b in spans[:i]:
                lane = lane + jnp.where((block >= a) & (block < b), 1, 0)
            row, to = plane_row(block), member(block)

            def act(key_rows, value_rows):
                pltpu.make_async_copy(key_rows, out.at[to, row, lane * 2], sem).start()
                pltpu.make_async_copy(value_rows, out.at[to, row, lane * 2 + 1], sem).start()

            block = start + block
            cached_block(core, h, block, (keys, values), (other_keys, other_values), True, act)
            return count + 2

        started = lax.fori_loop(first, last, one, started)
    wait_for(sem, started, out.at[0, 0, 0])


def first_call(info, cached, lanes):
    return pl.pallas_call(
        pack_first,
        out_shape=shaped(8, 4, lanes * 2, BLOCK, HD),
        in_specs=[SMEM, HBM, HBM, ANY, ANY],
        out_specs=VMEM,
        scratch_shapes=[pltpu.SemaphoreType.DMA],
        compiler_params=PARAMS,
        name="pack_first",
    )(info, *cached)


def pack_second(info, got, out):
    chip = info[0, CHIP]
    row_here = plane_row(chip)
    for end in ENDS:

        @pl.when(row_here == plane_row(end))
        def _(end=end):
            for zh in range(4):
                for h in range(KVS):
                    at = h * SLOTS + FREE * 2
                    out[zh, at : at + 2] = got[member(end), zh, 2 * h : 2 * h + 2]

    for zh in range(4):
        block = (chip & 25) + zh * 2
        sources = [(window(info, h, j) + block) >> 7 for h, j in PAIRS]
        for i, (h, j) in enumerate(PAIRS):

            @pl.when(plane_row(sources[i]) == row_here)
            def _(zh=zh, i=i, at=h * SLOTS + j * 2, sources=sources):
                source = sources[i]
                lane = jnp.where((source == ENDS[0]) | (source == ENDS[1]), KVS, 0)
                for before in sources[:i]:
                    lane = lane + jnp.where(before == source, 1, 0)
                out[zh, at : at + 2] = got[member(source), zh, pl.ds(lane * 2, 2)]


def second_call(info, got):
    return pl.pallas_call(
        pack_second,
        out_shape=shaped(4, KVS * SLOTS, BLOCK, HD),
        in_specs=[SMEM, VMEM],
        out_specs=VMEM,
        compiler_params=PARAMS,
        name="pack_second",
    )(info, got)


def pack_queries(core, queries, new_keys, new_values, send):
    other = 1 - core
    for g in range(GROUP):
        at = TRADED + g * OWN
        send[at : at + OWN] = queries[:, (other * GROUP + g) * HD : (other * GROUP + g + 1) * HD]
    at = TRADED + GROUP * OWN
    send[at : at + OWN] = new_keys[:, other * HD : (other + 1) * HD]
    send[at + OWN : at + 2 * OWN] = new_values[:, other * HD : (other + 1) * HD]


def finish_slash(info, got, queries, new_keys, new_values, keep, send):
    chip = info[0, CHIP]
    for h in range(KVS):
        for j in range(NS):
            if j < FREE:
                frm, slot = plane_row((window(info, h, j) + chip) >> 7), h * SLOTS + j * 2
            else:
                frm, slot = plane_row(ENDS[j - FREE]), h * SLOTS + FREE * 2
            if h == 0:
                keep[j] = got[frm, slot : slot + 2]
            else:
                send[j * 2 * BLOCK : (j * 2 + 1) * BLOCK] = got[frm, slot]
                send[(j * 2 + 1) * BLOCK : (j + 1) * 2 * BLOCK] = got[frm, slot + 1]
    pack_queries(0, queries, new_keys, new_values, send)


def finish_vertical(info, got, queries, new_keys, new_values, keep, send):
    for v in range(NV):
        keep[v] = got[v, 2:]
        send[v * 2 * BLOCK : (v * 2 + 1) * BLOCK] = got[v, 0]
        send[(v * 2 + 1) * BLOCK : (v + 1) * 2 * BLOCK] = got[v, 1]
    pack_queries(1, queries, new_keys, new_values, send)


def finish_call(kernel, info, got, rows):
    return pl.pallas_call(
        kernel,
        out_shape=(shaped(NV, 2, BLOCK, HD), shaped(TRADED + (GROUP + 2) * OWN, HD)),
        in_specs=[SMEM] + [VMEM] * 4,
        out_specs=(VMEM, VMEM),
        compiler_params=PARAMS,
        name=kernel.__name__,
    )(info, got, *rows)


def pack_vertical(info, keys, values, other_keys, other_values, out, sem):
    chip, core = info[0, CHIP], info[0, CORE]
    started = jnp.int32(0)
    for h in range(KVS):
        for v in range(NV):
            block = vertical_block(info, h, v)
            mine = (block >> 7) == chip

            def act(key_rows, value_rows, h=h, v=v):
                pltpu.make_async_copy(key_rows, out.at[v, 2 * h], sem).start()
                pltpu.make_async_copy(value_rows, out.at[v, 2 * h + 1], sem).start()

            cached_block(core, h, block, (keys, values), (other_keys, other_values), mine, act)
            started = started + jnp.where(mine, 2, 0)
    wait_for(sem, started, out.at[0, 0])


def pack_vertical_call(info, cached):
    return pl.pallas_call(
        pack_vertical,
        out_shape=shaped(NV, 2 * KVS, BLOCK, HD),
        in_specs=[SMEM, HBM, HBM, ANY, ANY],
        out_specs=VMEM,
        scratch_shapes=[pltpu.SemaphoreType.DMA],
        compiler_params=PARAMS,
        name="pack_vertical",
    )(info, *cached)


def spread_rows(info, got, out):
    here = member(info[0, CHIP])
    for h in range(KVS):
        mine = got[member(vertical_block(info, h, here) >> 7), 2 * h : 2 * h + 2]
        for to in range(4):
            out[to, 2 * h : 2 * h + 2] = mine


def spread_members(info, got, out):
    here = member(info[0, CHIP])
    for h in range(KVS):
        mine = got[plane_row(vertical_block(info, h, here) >> 7), 2 * h : 2 * h + 2]
        for to in range(NV):
            out[to, 2 * h : 2 * h + 2] = mine


def spread_call(kernel, copies, info, got):
    return pl.pallas_call(
        kernel,
        out_shape=shaped(copies, 2 * KVS, BLOCK, HD),
        in_specs=[SMEM, VMEM],
        out_specs=VMEM,
        compiler_params=PARAMS,
        name=kernel.__name__,
    )(info, got)


COLS = (NV + NS + 2) * BLOCK
CHUNK = 256


def attend(info, queries, new_keys, new_values, keep, theirs, out, keys, values, rows):
    chip, core = info[0, CHIP], info[0, CORE]
    ours = core == 0
    verticals, slashes = 0, NV * BLOCK

    @pl.when(ours)
    def _():
        for j in range(NS):
            at = slashes + j * BLOCK
            keys[at : at + BLOCK] = keep[j, 0]
            values[at : at + BLOCK] = keep[j, 1]
        for v in range(NV):
            at = verticals + v * BLOCK
            keys[at : at + BLOCK] = theirs[v * 2 * BLOCK : (v * 2 + 1) * BLOCK]
            values[at : at + BLOCK] = theirs[(v * 2 + 1) * BLOCK : (v + 1) * 2 * BLOCK]

    @pl.when(jnp.logical_not(ours))
    def _():
        for j in range(NS):
            at = slashes + j * BLOCK
            keys[at : at + BLOCK] = theirs[j * 2 * BLOCK : (j * 2 + 1) * BLOCK]
            values[at : at + BLOCK] = theirs[(j * 2 + 1) * BLOCK : (j + 1) * 2 * BLOCK]
        for v in range(NV):
            at = verticals + v * BLOCK
            keys[at : at + BLOCK] = keep[v, 0]
            values[at : at + BLOCK] = keep[v, 1]

    column = lax.broadcasted_iota(jnp.int32, (1, COLS), 1)
    allowed = column < (NV + NS) * BLOCK
    for j in range(NS):
        start = window(info, core, j) if j < FREE else (0, STORED - 32)[j - FREE]
        block = start + chip
        at = slashes + j * BLOCK
        repeated = jnp.int32(0)
        for v in range(NV):
            repeated = repeated | jnp.where(vertical_block(info, core, v) == block, 1, 0)
        here = (column >= at) & (column < at + BLOCK)
        allowed = allowed & jnp.logical_not(here & (repeated == 1))
    mine = pl.multiple_of(core * OWN, OWN)
    rest = pl.multiple_of((1 - core) * OWN, OWN)
    for g in range(GROUP):
        cols = pl.ds(pl.multiple_of((core * GROUP + g) * HD, HD), HD)
        rows[pl.ds(mine + g * BLOCK, OWN)] = queries[:, cols]
        at = TRADED + g * OWN
        rows[pl.ds(rest + g * BLOCK, OWN)] = theirs[at : at + OWN]
    at = (NV + NS) * BLOCK
    cols = pl.ds(pl.multiple_of(core * HD, HD), HD)
    fresh = TRADED + GROUP * OWN
    keys[pl.ds(mine + at, OWN)] = new_keys[:, cols]
    values[pl.ds(mine + at, OWN)] = new_values[:, cols]
    keys[pl.ds(rest + at, OWN)] = theirs[fresh : fresh + OWN]
    values[pl.ds(rest + at, OWN)] = theirs[fresh + OWN : fresh + 2 * OWN]
    keys[at + BLOCK :] = jnp.zeros((BLOCK, HD), jnp.bfloat16)
    values[at + BLOCK :] = jnp.zeros((BLOCK, HD), jnp.bfloat16)
    row = lax.broadcasted_iota(jnp.int32, (CHUNK, COLS), 0) & (BLOCK - 1)
    col = lax.broadcasted_iota(jnp.int32, (CHUNK, COLS), 1)
    own = (col >= at) & (col - at <= row) & (col < at + BLOCK)
    kept = own | allowed
    scale = math.log2(math.e) / math.sqrt(HD)
    per = CHUNK // BLOCK
    for pair in range(GROUP // per):
        scores = lax.dot_general(
            rows[pair * CHUNK : (pair + 1) * CHUNK],
            keys[...],
            (((1,), (1,)), ((), ())),
            preferred_element_type=jnp.float32,
        )
        scores = jnp.where(kept, scores, NEGATIVE)
        peak = jnp.max(scores, axis=-1, keepdims=True)
        weights = jnp.exp2((scores - peak) * scale)
        total = jnp.sum(weights, axis=-1, keepdims=True)
        acc = jnp.dot(
            weights.astype(jnp.bfloat16), values[...], preferred_element_type=jnp.float32
        )
        result = (acc / total).astype(jnp.bfloat16)
        for i in range(per):
            cols = slice((pair * per + i) * HD, (pair * per + i + 1) * HD)
            for c in range(2):
                for y in range(4):
                    r = i * BLOCK + c * 32 + y * 8
                    out[y * 2 + c, :, cols] = result[r : r + 8]


def attend_call(info, rows, keep, theirs):
    return pl.pallas_call(
        attend,
        out_shape=shaped(8, 8, GROUP * HD),
        in_specs=[SMEM] + [VMEM] * 5,
        out_specs=VMEM,
        scratch_shapes=[
            pltpu.VMEM((COLS, HD), jnp.bfloat16),
            pltpu.VMEM((COLS, HD), jnp.bfloat16),
            pltpu.VMEM((GROUP * BLOCK, HD), jnp.bfloat16),
        ],
        compiler_params=PARAMS,
        name="attend",
    )(info, *rows, keep, theirs)


def choice_of_lanes(slash):
    blocks = jnp.arange(32, dtype=jnp.int32)
    chips = ((STORED + blocks[None, None, :] - slash[:, :, None]) >> 7).reshape(KVS * NS, 32)
    same = jnp.sum((chips[:, None, :] == chips[None, :, :]).astype(jnp.int32), axis=1)
    most = jnp.max(same)
    return sum((most > lanes).astype(jnp.int32) for lanes in LANES[:-1])


def exchange(blocks, axes):
    return lax.all_to_all(blocks, axes, 0, 0, tiled=True)


def body(queries, cache_keys, cache_values, new_keys, new_values, vertical, slash):
    core = lax.axis_index("c").astype(jnp.int32)
    chip = (
        lax.axis_index("x") * 8 + lax.axis_index("zh") * 2 + lax.axis_index("zp")
    ).astype(jnp.int32)
    choice = choice_of_lanes(slash)
    here = jnp.broadcast_to(jnp.stack([chip, core, choice]), (2, 3))
    fixed = (slash == 32) | (slash == STORED)
    free = jnp.stack(
        [
            jnp.min(jnp.where(fixed, STORED, slash), axis=1),
            jnp.max(jnp.where(fixed, 32, slash), axis=1),
        ],
        axis=1,
    )
    info = jnp.concatenate([free, vertical, here], axis=1)
    rows = (queries, new_keys, new_values)
    swap = [(0, 1), (1, 0)]
    cached = (
        cache_keys,
        cache_values,
        lax.ppermute(cache_keys, "c", swap),
        lax.ppermute(cache_values, "c", swap),
    )
    cached = tuple(a.reshape(32, 2, BLOCK, KVS * HD) for a in cached)
    cached = tuple(pltpu.with_memory_space_constraint(a, pltpu.HBM) for a in cached[:2]) + cached[2:]

    def slashes():
        def through(lanes):
            return second_call(info, exchange(first_call(info, cached, lanes), ("x", "zp")))

        sent = lax.switch(choice, [functools.partial(through, lanes) for lanes in LANES])
        return finish_call(finish_slash, info, exchange(sent, "zh"), rows)

    def verticals():
        got = exchange(pack_vertical_call(info, cached), ("x", "zp"))
        got = exchange(spread_call(spread_rows, 4, info, got), "zh")
        got = exchange(spread_call(spread_members, NV, info, got), ("x", "zp"))
        return finish_call(finish_vertical, info, got, rows)

    keep, send = lax.cond(core == 0, slashes, verticals)
    theirs = lax.ppermute(send, "c", swap)
    out = attend_call(info, rows, keep, theirs)
    out = lax.all_to_all(out, ("y", "c"), 0, 0, tiled=True)
    return out.transpose(1, 0, 2).reshape(8, 8 * GROUP * HD)


def solution(mesh):
    parts = Mesh(mesh.devices.reshape(4, 4, 2, 2, 4), ("x", "zh", "zp", "c", "y"))
    ctx = ("x", "zh", "zp", "c")
    in_specs = (P(ctx, "y"),) * 5 + (P("y", None),) * 2
    out_specs = P(ctx + ("y",), None)
    return jax.shard_map(body, mesh=parts, in_specs=in_specs, out_specs=out_specs, check_vma=False)
```

```python
import functools
import math

import jax
import jax.numpy as jnp
from jax import lax
from jax.experimental import pallas as pl
from jax.experimental.pallas import tpu as pltpu
from jax.sharding import Mesh, PartitionSpec as P

HD = 128
BLOCK = 64
NV = 8
NS = 4
KVS = 2
GROUP = 8
STORED = 4096
PER_CHIP = 128
LANES = (2, 3, 4, 6)
NEGATIVE = -1e30
OWN = 32
SLOTS = (4, 5, 6)
FREE = 2
CHIP, CORE = FREE + NV, FREE + NV + 1
ENDS = (0, PER_CHIP // 4 - 1)
TRADED = NV * 2 * BLOCK
PAIRS = [(h, j) for h in range(KVS) for j in range(FREE)]

SMEM = pl.BlockSpec(memory_space=pltpu.SMEM)
HBM = pl.BlockSpec(memory_space=pltpu.HBM)
ANY = pl.BlockSpec(memory_space=pl.ANY)
VMEM = pl.BlockSpec(memory_space=pltpu.VMEM)
PARAMS = pltpu.CompilerParams(vmem_limit_bytes=32 * 1024 * 1024)


def shaped(*shape):
    return jax.ShapeDtypeStruct(shape, jnp.bfloat16)


def window(info, h, j):
    return STORED - info[h, j]


def vertical_block(info, h, v):
    return info[h, FREE + v]


def member(chip):
    return (chip >> 3) * 2 + (chip & 1)


def plane_row(chip):
    return (chip >> 1) & 3


END_ROWS = tuple(plane_row(end) for end in ENDS)


def wait_for(sem, count, like):
    def one(_, carry):
        pltpu.make_async_copy(like, like, sem).wait()
        return carry

    lax.fori_loop(0, count, one, 0)


def cached_block(core, h, block, mine, other, test, act):
    at = ((block >> 1) & 31, block & 1, slice(None), pl.ds(h * HD, HD))
    here = ((block >> 6) & 1) == core

    @pl.when(here & test)
    def _():
        act(mine[0].at[at], mine[1].at[at])

    @pl.when(jnp.logical_not(here) & test)
    def _():
        act(other[0].at[at], other[1].at[at])


def pack_first(info, keys, values, other_keys, other_values, out, sem):
    chip, core = info[0, CHIP], info[0, CORE]
    for end, pair, caches in (
        (ENDS[0], 0, (keys, values)),
        (ENDS[1], 16, (other_keys, other_values)),
    ):

        @pl.when(chip == end)
        def _(pair=pair, caches=caches):
            copies = []
            for to in range(8):
                pairs = pl.ds(pair + (to >> 1) * 4, 4)
                for h in range(KVS):
                    for k, cache in enumerate(caches):
                        copies.append(
                            pltpu.make_async_copy(
                                cache.at[pairs, to & 1, :, pl.ds(h * HD, HD)],
                                out.at[to, :, 2 * h + k],
                                sem,
                            )
                        )
            for c in copies:
                c.start()
            for c in copies:
                c.wait()

    base = jnp.where((chip == ENDS[0]) | (chip == ENDS[1]), KVS, 0)
    spans = []
    for h, j in PAIRS:
        start = window(info, h, j)
        first = jnp.clip(chip * PER_CHIP - start, 0, 32)
        last = jnp.clip((chip + 1) * PER_CHIP - start, 0, 32)
        spans.append((start, first, last))
    started = jnp.int32(0)
    for i, (h, _) in enumerate(PAIRS):
        start, first, last = spans[i]

        def one(block, count, i=i, h=h, start=start):
            lane = base
            for _, a, b in spans[:i]:
                lane = lane + jnp.where((block >= a) & (block < b), 1, 0)
            row, to = plane_row(block), member(block)

            def act(key_rows, value_rows):
                pltpu.make_async_copy(key_rows, out.at[to, row, lane * 2], sem).start()
                pltpu.make_async_copy(value_rows, out.at[to, row, lane * 2 + 1], sem).start()

            block = start + block
            cached_block(core, h, block, (keys, values), (other_keys, other_values), True, act)
            return count + 2

        started = lax.fori_loop(first, last, one, started)
    wait_for(sem, started, out.at[0, 0, 0])


def first_call(info, cached, lanes):
    return pl.pallas_call(
        pack_first,
        out_shape=shaped(8, 4, lanes * 2, BLOCK, HD),
        in_specs=[SMEM, HBM, HBM, ANY, ANY],
        out_specs=VMEM,
        scratch_shapes=[pltpu.SemaphoreType.DMA],
        compiler_params=PARAMS,
        name="pack_first",
    )(info, *cached)


def sources_of(info, block):
    return [(window(info, h, j) + block) >> 7 for h, j in PAIRS]


def rank_of(i, keys, fixed):
    rank = jnp.where((keys[i] == fixed[0]) | (keys[i] == fixed[1]), KVS, 0)
    for before in keys[:i]:
        rank = rank + jnp.where(before == keys[i], 1, 0)
    return rank


def pack_second(info, got, out):
    chip = info[0, CHIP]
    row_here = plane_row(chip)
    for end in ENDS:

        @pl.when(row_here == plane_row(end))
        def _(end=end):
            for zh in range(4):
                out[zh, : 2 * KVS] = got[member(end), zh, : 2 * KVS]

    for zh in range(4):
        sources = sources_of(info, (chip & 25) + zh * 2)
        rows = [plane_row(source) for source in sources]
        for i in range(len(PAIRS)):

            @pl.when(rows[i] == row_here)
            def _(zh=zh, i=i, sources=sources, rows=rows):
                lane = rank_of(i, sources, ENDS)
                slot = rank_of(i, rows, END_ROWS)
                out[zh, pl.ds(slot * 2, 2)] = got[member(sources[i]), zh, pl.ds(lane * 2, 2)]


def second_call(info, got, slots):
    return pl.pallas_call(
        pack_second,
        out_shape=shaped(4, slots * 2, BLOCK, HD),
        in_specs=[SMEM, VMEM],
        out_specs=VMEM,
        compiler_params=PARAMS,
        name="pack_second",
    )(info, got)


def pack_queries(core, queries, new_keys, new_values, send):
    other = 1 - core
    for g in range(GROUP):
        at = TRADED + g * OWN
        send[at : at + OWN] = queries[:, (other * GROUP + g) * HD : (other * GROUP + g + 1) * HD]
    at = TRADED + GROUP * OWN
    send[at : at + OWN] = new_keys[:, other * HD : (other + 1) * HD]
    send[at + OWN : at + 2 * OWN] = new_values[:, other * HD : (other + 1) * HD]


def finish_slash(info, got, queries, new_keys, new_values, keep, send):
    rows = [plane_row(source) for source in sources_of(info, info[0, CHIP])]
    for h in range(KVS):
        for j in range(NS):
            if j < FREE:
                i = PAIRS.index((h, j))
                frm, slot = rows[i], rank_of(i, rows, END_ROWS) * 2
            else:
                frm, slot = END_ROWS[j - FREE], h * 2
            if h == 0:
                keep[j] = got[frm, pl.ds(slot, 2)]
            else:
                send[j * 2 * BLOCK : (j * 2 + 1) * BLOCK] = got[frm, slot]
                send[(j * 2 + 1) * BLOCK : (j + 1) * 2 * BLOCK] = got[frm, slot + 1]
    pack_queries(0, queries, new_keys, new_values, send)


def finish_vertical(info, got, queries, new_keys, new_values, keep, send):
    for v in range(NV):
        keep[v] = got[v, 2:]
        send[v * 2 * BLOCK : (v * 2 + 1) * BLOCK] = got[v, 0]
        send[(v * 2 + 1) * BLOCK : (v + 1) * 2 * BLOCK] = got[v, 1]
    pack_queries(1, queries, new_keys, new_values, send)


def finish_call(kernel, info, got, rows):
    return pl.pallas_call(
        kernel,
        out_shape=(shaped(NV, 2, BLOCK, HD), shaped(TRADED + (GROUP + 2) * OWN, HD)),
        in_specs=[SMEM] + [VMEM] * 4,
        out_specs=(VMEM, VMEM),
        compiler_params=PARAMS,
        name=kernel.__name__,
    )(info, got, *rows)


def pack_vertical(info, keys, values, other_keys, other_values, out, sem):
    chip, core = info[0, CHIP], info[0, CORE]
    started = jnp.int32(0)
    for h in range(KVS):
        for v in range(NV):
            block = vertical_block(info, h, v)
            mine = (block >> 7) == chip

            def act(key_rows, value_rows, h=h, v=v):
                pltpu.make_async_copy(key_rows, out.at[v, 2 * h], sem).start()
                pltpu.make_async_copy(value_rows, out.at[v, 2 * h + 1], sem).start()

            cached_block(core, h, block, (keys, values), (other_keys, other_values), mine, act)
            started = started + jnp.where(mine, 2, 0)
    wait_for(sem, started, out.at[0, 0])


def pack_vertical_call(info, cached):
    return pl.pallas_call(
        pack_vertical,
        out_shape=shaped(NV, 2 * KVS, BLOCK, HD),
        in_specs=[SMEM, HBM, HBM, ANY, ANY],
        out_specs=VMEM,
        scratch_shapes=[pltpu.SemaphoreType.DMA],
        compiler_params=PARAMS,
        name="pack_vertical",
    )(info, *cached)


def spread_rows(info, got, out):
    here = member(info[0, CHIP])
    for h in range(KVS):
        mine = got[member(vertical_block(info, h, here) >> 7), 2 * h : 2 * h + 2]
        for to in range(4):
            out[to, 2 * h : 2 * h + 2] = mine


def spread_members(info, got, out):
    here = member(info[0, CHIP])
    for h in range(KVS):
        mine = got[plane_row(vertical_block(info, h, here) >> 7), 2 * h : 2 * h + 2]
        for to in range(NV):
            out[to, 2 * h : 2 * h + 2] = mine


def spread_call(kernel, copies, info, got):
    return pl.pallas_call(
        kernel,
        out_shape=shaped(copies, 2 * KVS, BLOCK, HD),
        in_specs=[SMEM, VMEM],
        out_specs=VMEM,
        compiler_params=PARAMS,
        name=kernel.__name__,
    )(info, got)


COLS = (NV + NS + 2) * BLOCK
CHUNK = 256


def attend(info, queries, new_keys, new_values, keep, theirs, out, keys, values, rows):
    chip, core = info[0, CHIP], info[0, CORE]
    ours = core == 0
    verticals, slashes = 0, NV * BLOCK

    @pl.when(ours)
    def _():
        for j in range(NS):
            at = slashes + j * BLOCK
            keys[at : at + BLOCK] = keep[j, 0]
            values[at : at + BLOCK] = keep[j, 1]
        for v in range(NV):
            at = verticals + v * BLOCK
            keys[at : at + BLOCK] = theirs[v * 2 * BLOCK : (v * 2 + 1) * BLOCK]
            values[at : at + BLOCK] = theirs[(v * 2 + 1) * BLOCK : (v + 1) * 2 * BLOCK]

    @pl.when(jnp.logical_not(ours))
    def _():
        for j in range(NS):
            at = slashes + j * BLOCK
            keys[at : at + BLOCK] = theirs[j * 2 * BLOCK : (j * 2 + 1) * BLOCK]
            values[at : at + BLOCK] = theirs[(j * 2 + 1) * BLOCK : (j + 1) * 2 * BLOCK]
        for v in range(NV):
            at = verticals + v * BLOCK
            keys[at : at + BLOCK] = keep[v, 0]
            values[at : at + BLOCK] = keep[v, 1]

    column = lax.broadcasted_iota(jnp.int32, (1, COLS), 1)
    allowed = column < (NV + NS) * BLOCK
    for j in range(NS):
        start = window(info, core, j) if j < FREE else (0, STORED - 32)[j - FREE]
        block = start + chip
        at = slashes + j * BLOCK
        repeated = jnp.int32(0)
        for v in range(NV):
            repeated = repeated | jnp.where(vertical_block(info, core, v) == block, 1, 0)
        here = (column >= at) & (column < at + BLOCK)
        allowed = allowed & jnp.logical_not(here & (repeated == 1))
    mine = pl.multiple_of(core * OWN, OWN)
    rest = pl.multiple_of((1 - core) * OWN, OWN)
    for g in range(GROUP):
        cols = pl.ds(pl.multiple_of((core * GROUP + g) * HD, HD), HD)
        rows[pl.ds(mine + g * BLOCK, OWN)] = queries[:, cols]
        at = TRADED + g * OWN
        rows[pl.ds(rest + g * BLOCK, OWN)] = theirs[at : at + OWN]
    at = (NV + NS) * BLOCK
    cols = pl.ds(pl.multiple_of(core * HD, HD), HD)
    fresh = TRADED + GROUP * OWN
    keys[pl.ds(mine + at, OWN)] = new_keys[:, cols]
    values[pl.ds(mine + at, OWN)] = new_values[:, cols]
    keys[pl.ds(rest + at, OWN)] = theirs[fresh : fresh + OWN]
    values[pl.ds(rest + at, OWN)] = theirs[fresh + OWN : fresh + 2 * OWN]
    keys[at + BLOCK :] = jnp.zeros((BLOCK, HD), jnp.bfloat16)
    values[at + BLOCK :] = jnp.zeros((BLOCK, HD), jnp.bfloat16)
    row = lax.broadcasted_iota(jnp.int32, (CHUNK, COLS), 0) & (BLOCK - 1)
    col = lax.broadcasted_iota(jnp.int32, (CHUNK, COLS), 1)
    own = (col >= at) & (col - at <= row) & (col < at + BLOCK)
    kept = own | allowed
    scale = math.log2(math.e) / math.sqrt(HD)
    per = CHUNK // BLOCK
    for pair in range(GROUP // per):
        scores = lax.dot_general(
            rows[pair * CHUNK : (pair + 1) * CHUNK],
            keys[...],
            (((1,), (1,)), ((), ())),
            preferred_element_type=jnp.float32,
        )
        scores = jnp.where(kept, scores, NEGATIVE)
        peak = jnp.max(scores, axis=-1, keepdims=True)
        weights = jnp.exp2((scores - peak) * scale)
        total = jnp.sum(weights, axis=-1, keepdims=True)
        acc = jnp.dot(
            weights.astype(jnp.bfloat16), values[...], preferred_element_type=jnp.float32
        )
        result = (acc / total).astype(jnp.bfloat16)
        for i in range(per):
            cols = slice((pair * per + i) * HD, (pair * per + i + 1) * HD)
            for c in range(2):
                for y in range(4):
                    r = i * BLOCK + c * 32 + y * 8
                    out[y * 2 + c, :, cols] = result[r : r + 8]


def attend_call(info, rows, keep, theirs):
    return pl.pallas_call(
        attend,
        out_shape=shaped(8, 8, GROUP * HD),
        in_specs=[SMEM] + [VMEM] * 5,
        out_specs=VMEM,
        scratch_shapes=[
            pltpu.VMEM((COLS, HD), jnp.bfloat16),
            pltpu.VMEM((COLS, HD), jnp.bfloat16),
            pltpu.VMEM((GROUP * BLOCK, HD), jnp.bfloat16),
        ],
        compiler_params=PARAMS,
        name="attend",
    )(info, *rows, keep, theirs)


def choice_of(slash):
    blocks = jnp.arange(32, dtype=jnp.int32)
    chips = ((STORED + blocks[None, None, :] - slash[:, :, None]) >> 7).reshape(KVS * NS, 32)
    chosen = jnp.int32(0)
    for keys, sizes in ((chips, LANES), (plane_row(chips), SLOTS)):
        most = jnp.max(jnp.sum((keys[:, None, :] == keys[None, :, :]).astype(jnp.int32), axis=1))
        chosen = chosen * len(sizes) + sum((most > n).astype(jnp.int32) for n in sizes[:-1])
    return chosen


def exchange(blocks, axes):
    return lax.all_to_all(blocks, axes, 0, 0, tiled=True)


def body(queries, cache_keys, cache_values, new_keys, new_values, vertical, slash):
    core = lax.axis_index("c").astype(jnp.int32)
    chip = (
        lax.axis_index("x") * 8 + lax.axis_index("zh") * 2 + lax.axis_index("zp")
    ).astype(jnp.int32)
    choice = choice_of(slash)
    here = jnp.broadcast_to(jnp.stack([chip, core, choice]), (2, 3))
    fixed = (slash == 32) | (slash == STORED)
    free = jnp.stack(
        [
            jnp.min(jnp.where(fixed, STORED, slash), axis=1),
            jnp.max(jnp.where(fixed, 32, slash), axis=1),
        ],
        axis=1,
    )
    info = jnp.concatenate([free, vertical, here], axis=1)
    rows = (queries, new_keys, new_values)
    swap = [(0, 1), (1, 0)]
    cached = (
        cache_keys,
        cache_values,
        lax.ppermute(cache_keys, "c", swap),
        lax.ppermute(cache_values, "c", swap),
    )
    cached = tuple(a.reshape(32, 2, BLOCK, KVS * HD) for a in cached)
    cached = tuple(pltpu.with_memory_space_constraint(a, pltpu.HBM) for a in cached[:2]) + cached[2:]

    def slashes(lanes, slots):
        got = exchange(first_call(info, cached, lanes), ("x", "zp"))
        got = exchange(second_call(info, got, slots), "zh")
        return finish_call(finish_slash, info, got, rows)

    def verticals():
        got = exchange(pack_vertical_call(info, cached), ("x", "zp"))
        got = exchange(spread_call(spread_rows, 4, info, got), "zh")
        got = exchange(spread_call(spread_members, NV, info, got), ("x", "zp"))
        return finish_call(finish_vertical, info, got, rows)

    ways = [functools.partial(slashes, n, m) for n in LANES for m in SLOTS]
    keep, send = lax.switch(jnp.where(core == 0, 1 + choice, 0), [verticals] + ways)
    theirs = lax.ppermute(send, "c", swap)
    out = attend_call(info, rows, keep, theirs)
    out = lax.all_to_all(out, ("y", "c"), 0, 0, tiled=True)
    return out.transpose(1, 0, 2).reshape(8, 8 * GROUP * HD)


def solution(mesh):
    parts = Mesh(mesh.devices.reshape(4, 4, 2, 2, 4), ("x", "zh", "zp", "c", "y"))
    ctx = ("x", "zh", "zp", "c")
    in_specs = (P(ctx, "y"),) * 5 + (P("y", None),) * 2
    out_specs = P(ctx + ("y",), None)
    return jax.shard_map(body, mesh=parts, in_specs=in_specs, out_specs=out_specs, check_vma=False)
```

```python
import functools
import math

import jax
import jax.numpy as jnp
from jax import lax
from jax.experimental import pallas as pl
from jax.experimental.pallas import tpu as pltpu
from jax.sharding import Mesh, PartitionSpec as P

HD = 128
BLOCK = 64
NV = 8
NS = 4
KVS = 2
GROUP = 8
STORED = 4096
PER_CHIP = 128
LANES = (2, 3, 4, 6)
NEGATIVE = -1e30
OWN = 32
SLOTS = (4, 5, 6)
FREE = 2
CHIP, CORE = FREE + NV, FREE + NV + 1
ENDS = (0, PER_CHIP // 4 - 1)
TRADED = NV * 2 * BLOCK
PAIRS = [(h, j) for h in range(KVS) for j in range(FREE)]

SMEM = pl.BlockSpec(memory_space=pltpu.SMEM)
HBM = pl.BlockSpec(memory_space=pltpu.HBM)
ANY = pl.BlockSpec(memory_space=pl.ANY)
VMEM = pl.BlockSpec(memory_space=pltpu.VMEM)
PARAMS = pltpu.CompilerParams(vmem_limit_bytes=32 * 1024 * 1024)


def shaped(*shape):
    return jax.ShapeDtypeStruct(shape, jnp.bfloat16)


def window(info, h, j):
    return STORED - info[h, j]


def vertical_block(info, h, v):
    return info[h, FREE + v]


def member(chip):
    return (chip >> 3) * 2 + (chip & 1)


def plane_row(chip):
    return (chip >> 1) & 3


END_ROWS = tuple(plane_row(end) for end in ENDS)


def wait_for(sem, count, like):
    def one(_, carry):
        pltpu.make_async_copy(like, like, sem).wait()
        return carry

    lax.fori_loop(0, count, one, 0)


def cached_block(core, h, block, mine, other, test, act):
    at = ((block >> 1) & 31, block & 1, slice(None), pl.ds(h * HD, HD))
    here = ((block >> 6) & 1) == core

    @pl.when(here & test)
    def _():
        act(mine[0].at[at], mine[1].at[at])

    @pl.when(jnp.logical_not(here) & test)
    def _():
        act(other[0].at[at], other[1].at[at])


def pack_first(info, keys, values, other_keys, other_values, out, sem):
    chip, core = info[0, CHIP], info[0, CORE]
    for end, pair, caches in (
        (ENDS[0], 0, (keys, values)),
        (ENDS[1], 16, (other_keys, other_values)),
    ):

        @pl.when(chip == end)
        def _(pair=pair, caches=caches):
            copies = []
            for to in range(8):
                pairs = pl.ds(pair + (to >> 1) * 4, 4)
                for h in range(KVS):
                    for k, cache in enumerate(caches):
                        copies.append(
                            pltpu.make_async_copy(
                                cache.at[pairs, to & 1, :, pl.ds(h * HD, HD)],
                                out.at[to, :, 2 * h + k],
                                sem,
                            )
                        )
            for c in copies:
                c.start()
            for c in copies:
                c.wait()

    base = jnp.where((chip == ENDS[0]) | (chip == ENDS[1]), KVS, 0)
    spans = []
    for h, j in PAIRS:
        start = window(info, h, j)
        first = jnp.clip(chip * PER_CHIP - start, 0, 32)
        last = jnp.clip((chip + 1) * PER_CHIP - start, 0, 32)
        spans.append((start, first, last))
    started = jnp.int32(0)
    for i, (h, _) in enumerate(PAIRS):
        start, first, last = spans[i]

        def one(block, count, i=i, h=h, start=start):
            lane = base
            for _, a, b in spans[:i]:
                lane = lane + jnp.where((block >= a) & (block < b), 1, 0)
            row, to = plane_row(block), member(block)

            def act(key_rows, value_rows):
                pltpu.make_async_copy(key_rows, out.at[to, row, lane * 2], sem).start()
                pltpu.make_async_copy(value_rows, out.at[to, row, lane * 2 + 1], sem).start()

            block = start + block
            cached_block(core, h, block, (keys, values), (other_keys, other_values), True, act)
            return count + 2

        started = lax.fori_loop(first, last, one, started)
    wait_for(sem, started, out.at[0, 0, 0])


def first_call(info, cached, lanes):
    return pl.pallas_call(
        pack_first,
        out_shape=shaped(8, 4, lanes * 2, BLOCK, HD),
        in_specs=[SMEM, HBM, HBM, ANY, ANY],
        out_specs=VMEM,
        scratch_shapes=[pltpu.SemaphoreType.DMA],
        compiler_params=PARAMS,
        name="pack_first",
    )(info, *cached)


def sources_of(info, block):
    return [(window(info, h, j) + block) >> 7 for h, j in PAIRS]


def rank_of(i, keys, fixed):
    rank = jnp.where((keys[i] == fixed[0]) | (keys[i] == fixed[1]), KVS, 0)
    for before in keys[:i]:
        rank = rank + jnp.where(before == keys[i], 1, 0)
    return rank


def pack_second(info, got, out):
    chip = info[0, CHIP]
    row_here = plane_row(chip)
    for end in ENDS:

        @pl.when(row_here == plane_row(end))
        def _(end=end):
            for zh in range(4):
                out[zh, : 2 * KVS] = got[member(end), zh, : 2 * KVS]

    for zh in range(4):
        sources = sources_of(info, (chip & 25) + zh * 2)
        rows = [plane_row(source) for source in sources]
        for i in range(len(PAIRS)):

            @pl.when(rows[i] == row_here)
            def _(zh=zh, i=i, sources=sources, rows=rows):
                lane = rank_of(i, sources, ENDS)
                slot = rank_of(i, rows, END_ROWS)
                out[zh, pl.ds(slot * 2, 2)] = got[member(sources[i]), zh, pl.ds(lane * 2, 2)]


def second_call(info, got, slots):
    return pl.pallas_call(
        pack_second,
        out_shape=shaped(4, slots * 2, BLOCK, HD),
        in_specs=[SMEM, VMEM],
        out_specs=VMEM,
        compiler_params=PARAMS,
        name="pack_second",
    )(info, got)


def pack_queries(core, queries, new_keys, new_values, send):
    other = 1 - core
    for g in range(GROUP):
        at = TRADED + g * OWN
        send[at : at + OWN] = queries[:, (other * GROUP + g) * HD : (other * GROUP + g + 1) * HD]
    at = TRADED + GROUP * OWN
    send[at : at + OWN] = new_keys[:, other * HD : (other + 1) * HD]
    send[at + OWN : at + 2 * OWN] = new_values[:, other * HD : (other + 1) * HD]


def finish_slash(info, got, queries, new_keys, new_values, keep, send):
    rows = [plane_row(source) for source in sources_of(info, info[0, CHIP])]
    for h in range(KVS):
        for j in range(NS):
            if j < FREE:
                i = PAIRS.index((h, j))
                frm, slot = rows[i], rank_of(i, rows, END_ROWS) * 2
            else:
                frm, slot = END_ROWS[j - FREE], h * 2
            if h == 0:
                keep[j] = got[frm, pl.ds(slot, 2)]
            else:
                send[j * 2 * BLOCK : (j * 2 + 1) * BLOCK] = got[frm, slot]
                send[(j * 2 + 1) * BLOCK : (j + 1) * 2 * BLOCK] = got[frm, slot + 1]
    pack_queries(0, queries, new_keys, new_values, send)


def finish_vertical(info, got, queries, new_keys, new_values, keep, send):
    for v in range(NV):
        keep[v] = got[v, 2:]
        send[v * 2 * BLOCK : (v * 2 + 1) * BLOCK] = got[v, 0]
        send[(v * 2 + 1) * BLOCK : (v + 1) * 2 * BLOCK] = got[v, 1]
    pack_queries(1, queries, new_keys, new_values, send)


def finish_call(kernel, info, got, rows):
    return pl.pallas_call(
        kernel,
        out_shape=(shaped(NV, 2, BLOCK, HD), shaped(TRADED + (GROUP + 2) * OWN, HD)),
        in_specs=[SMEM] + [VMEM] * 4,
        out_specs=(VMEM, VMEM),
        compiler_params=PARAMS,
        name=kernel.__name__,
    )(info, got, *rows)


def pack_vertical(info, keys, values, other_keys, other_values, out, sem):
    chip, core = info[0, CHIP], info[0, CORE]
    started = jnp.int32(0)
    for h in range(KVS):
        for v in range(NV):
            block = vertical_block(info, h, v)
            mine = (block >> 7) == chip

            def act(key_rows, value_rows, h=h, v=v):
                pltpu.make_async_copy(key_rows, out.at[v, 2 * h], sem).start()
                pltpu.make_async_copy(value_rows, out.at[v, 2 * h + 1], sem).start()

            cached_block(core, h, block, (keys, values), (other_keys, other_values), mine, act)
            started = started + jnp.where(mine, 2, 0)
    wait_for(sem, started, out.at[0, 0])


def pack_vertical_call(info, cached):
    return pl.pallas_call(
        pack_vertical,
        out_shape=shaped(NV, 2 * KVS, BLOCK, HD),
        in_specs=[SMEM, HBM, HBM, ANY, ANY],
        out_specs=VMEM,
        scratch_shapes=[pltpu.SemaphoreType.DMA],
        compiler_params=PARAMS,
        name="pack_vertical",
    )(info, *cached)


def spread_rows(info, got, out):
    here = member(info[0, CHIP])
    for h in range(KVS):
        mine = got[member(vertical_block(info, h, here) >> 7), 2 * h : 2 * h + 2]
        for to in range(4):
            out[to, 2 * h : 2 * h + 2] = mine


def spread_members(info, got, out):
    here = member(info[0, CHIP])
    for h in range(KVS):
        mine = got[plane_row(vertical_block(info, h, here) >> 7), 2 * h : 2 * h + 2]
        for to in range(NV):
            out[to, 2 * h : 2 * h + 2] = mine


def spread_call(kernel, copies, info, got):
    return pl.pallas_call(
        kernel,
        out_shape=shaped(copies, 2 * KVS, BLOCK, HD),
        in_specs=[SMEM, VMEM],
        out_specs=VMEM,
        compiler_params=PARAMS,
        name=kernel.__name__,
    )(info, got)


COLS = (NV + NS + 2) * BLOCK
CHUNK = 256


def attend(info, queries, new_keys, new_values, keep, theirs, out, keys, values, rows):
    chip, core = info[0, CHIP], info[0, CORE]
    ours = core == 0
    verticals, slashes = 0, NV * BLOCK

    @pl.when(ours)
    def _():
        for j in range(NS):
            at = slashes + j * BLOCK
            keys[at : at + BLOCK] = keep[j, 0]
            values[at : at + BLOCK] = keep[j, 1]
        for v in range(NV):
            at = verticals + v * BLOCK
            keys[at : at + BLOCK] = theirs[v * 2 * BLOCK : (v * 2 + 1) * BLOCK]
            values[at : at + BLOCK] = theirs[(v * 2 + 1) * BLOCK : (v + 1) * 2 * BLOCK]

    @pl.when(jnp.logical_not(ours))
    def _():
        for j in range(NS):
            at = slashes + j * BLOCK
            keys[at : at + BLOCK] = theirs[j * 2 * BLOCK : (j * 2 + 1) * BLOCK]
            values[at : at + BLOCK] = theirs[(j * 2 + 1) * BLOCK : (j + 1) * 2 * BLOCK]
        for v in range(NV):
            at = verticals + v * BLOCK
            keys[at : at + BLOCK] = keep[v, 0]
            values[at : at + BLOCK] = keep[v, 1]

    column = lax.broadcasted_iota(jnp.int32, (1, COLS), 1)
    allowed = column < (NV + NS) * BLOCK
    for j in range(NS):
        start = window(info, core, j) if j < FREE else (0, STORED - 32)[j - FREE]
        block = start + chip
        at = slashes + j * BLOCK
        repeated = jnp.int32(0)
        for v in range(NV):
            repeated = repeated | jnp.where(vertical_block(info, core, v) == block, 1, 0)
        here = (column >= at) & (column < at + BLOCK)
        allowed = allowed & jnp.logical_not(here & (repeated == 1))
    mine = pl.multiple_of(core * OWN, OWN)
    rest = pl.multiple_of((1 - core) * OWN, OWN)
    for g in range(GROUP):
        cols = pl.ds(pl.multiple_of((core * GROUP + g) * HD, HD), HD)
        rows[pl.ds(mine + g * BLOCK, OWN)] = queries[:, cols]
        at = TRADED + g * OWN
        rows[pl.ds(rest + g * BLOCK, OWN)] = theirs[at : at + OWN]
    at = (NV + NS) * BLOCK
    cols = pl.ds(pl.multiple_of(core * HD, HD), HD)
    fresh = TRADED + GROUP * OWN
    keys[pl.ds(mine + at, OWN)] = new_keys[:, cols]
    values[pl.ds(mine + at, OWN)] = new_values[:, cols]
    keys[pl.ds(rest + at, OWN)] = theirs[fresh : fresh + OWN]
    values[pl.ds(rest + at, OWN)] = theirs[fresh + OWN : fresh + 2 * OWN]
    keys[at + BLOCK :] = jnp.zeros((BLOCK, HD), jnp.bfloat16)
    values[at + BLOCK :] = jnp.zeros((BLOCK, HD), jnp.bfloat16)
    row = lax.broadcasted_iota(jnp.int32, (CHUNK, COLS), 0) & (BLOCK - 1)
    col = lax.broadcasted_iota(jnp.int32, (CHUNK, COLS), 1)
    own = (col >= at) & (col - at <= row) & (col < at + BLOCK)
    kept = own | allowed
    scale = math.log2(math.e) / math.sqrt(HD)
    per = CHUNK // BLOCK
    for pair in range(GROUP // per):
        scores = lax.dot_general(
            rows[pair * CHUNK : (pair + 1) * CHUNK],
            keys[...],
            (((1,), (1,)), ((), ())),
            preferred_element_type=jnp.float32,
        )
        scores = jnp.where(kept, scores, NEGATIVE)
        peak = jnp.max(scores, axis=-1, keepdims=True)
        weights = jnp.exp2((scores - peak) * scale)
        total = jnp.sum(weights, axis=-1, keepdims=True)
        acc = jnp.dot(
            weights.astype(jnp.bfloat16), values[...], preferred_element_type=jnp.float32
        )
        result = (acc / total).astype(jnp.bfloat16)
        for i in range(per):
            cols = slice((pair * per + i) * HD, (pair * per + i + 1) * HD)
            for c in range(2):
                for y in range(4):
                    r = i * BLOCK + c * 32 + y * 8
                    out[y * 2 + c, :, cols] = result[r : r + 8]


def attend_call(info, rows, keep, theirs):
    return pl.pallas_call(
        attend,
        out_shape=shaped(8, 8, GROUP * HD),
        in_specs=[SMEM] + [VMEM] * 5,
        out_specs=VMEM,
        scratch_shapes=[
            pltpu.VMEM((COLS, HD), jnp.bfloat16),
            pltpu.VMEM((COLS, HD), jnp.bfloat16),
            pltpu.VMEM((GROUP * BLOCK, HD), jnp.bfloat16),
        ],
        compiler_params=PARAMS,
        name="attend",
    )(info, *rows, keep, theirs)


def choice_of(slash):
    blocks = jnp.arange(32, dtype=jnp.int32)
    chips = ((STORED + blocks[None, None, :] - slash[:, :, None]) >> 7).reshape(KVS * NS, 32)
    keys = jnp.stack([chips, plane_row(chips)])
    same = (keys[:, :, None, :] == keys[:, None, :, :]).astype(jnp.int32)
    most = jnp.max(jnp.sum(same, axis=2), axis=(1, 2))
    chosen = jnp.int32(0)
    for i, sizes in enumerate((LANES, SLOTS)):
        chosen = chosen * len(sizes) + sum((most[i] > n).astype(jnp.int32) for n in sizes[:-1])
    return chosen


def exchange(blocks, axes):
    return lax.all_to_all(blocks, axes, 0, 0, tiled=True)


def body(queries, cache_keys, cache_values, new_keys, new_values, vertical, slash):
    core = lax.axis_index("c").astype(jnp.int32)
    chip = (
        lax.axis_index("x") * 8 + lax.axis_index("zh") * 2 + lax.axis_index("zp")
    ).astype(jnp.int32)
    choice = choice_of(slash)
    here = jnp.broadcast_to(jnp.stack([chip, core, choice]), (2, 3))
    fixed = (slash == 32) | (slash == STORED)
    free = jnp.stack(
        [
            jnp.min(jnp.where(fixed, STORED, slash), axis=1),
            jnp.max(jnp.where(fixed, 32, slash), axis=1),
        ],
        axis=1,
    )
    info = jnp.concatenate([free, vertical, here], axis=1)
    rows = (queries, new_keys, new_values)
    swap = [(0, 1), (1, 0)]
    cached = (
        cache_keys,
        cache_values,
        lax.ppermute(cache_keys, "c", swap),
        lax.ppermute(cache_values, "c", swap),
    )
    cached = tuple(a.reshape(32, 2, BLOCK, KVS * HD) for a in cached)
    cached = tuple(pltpu.with_memory_space_constraint(a, pltpu.HBM) for a in cached[:2]) + cached[2:]

    def slashes(lanes, slots):
        got = exchange(first_call(info, cached, lanes), ("x", "zp"))
        got = exchange(second_call(info, got, slots), "zh")
        return finish_call(finish_slash, info, got, rows)

    def verticals():
        got = exchange(pack_vertical_call(info, cached), ("x", "zp"))
        got = exchange(spread_call(spread_rows, 4, info, got), "zh")
        got = exchange(spread_call(spread_members, NV, info, got), ("x", "zp"))
        return finish_call(finish_vertical, info, got, rows)

    ways = [functools.partial(slashes, n, m) for n in LANES for m in SLOTS]
    keep, send = lax.switch(jnp.where(core == 0, 1 + choice, 0), [verticals] + ways)
    theirs = lax.ppermute(send, "c", swap)
    out = attend_call(info, rows, keep, theirs)
    out = lax.all_to_all(out, ("y", "c"), 0, 0, tiled=True)
    return out.transpose(1, 0, 2).reshape(8, 8 * GROUP * HD)


def solution(mesh):
    parts = Mesh(mesh.devices.reshape(4, 4, 2, 2, 4), ("x", "zh", "zp", "c", "y"))
    ctx = ("x", "zh", "zp", "c")
    in_specs = (P(ctx, "y"),) * 5 + (P("y", None),) * 2
    out_specs = P(ctx + ("y",), None)
    return jax.shard_map(body, mesh=parts, in_specs=in_specs, out_specs=out_specs, check_vma=False)
```

```python
import functools
import math

import jax
import jax.numpy as jnp
from jax import lax
from jax.experimental import pallas as pl
from jax.experimental.pallas import tpu as pltpu
from jax.sharding import Mesh, PartitionSpec as P

HD = 128
BLOCK = 64
NV = 8
NS = 4
KVS = 2
GROUP = 8
STORED = 4096
PER_CHIP = 128
LANES = (2, 3, 4, 6)
NEGATIVE = -1e30
OWN = 32
SLOTS = (4, 5, 6)
FREE = 2
CHIP, CORE = FREE + NV, FREE + NV + 1
ENDS = (0, PER_CHIP // 4 - 1)
TRADED = NV * 2 * BLOCK
PAIRS = [(h, j) for h in range(KVS) for j in range(FREE)]

SMEM = pl.BlockSpec(memory_space=pltpu.SMEM)
HBM = pl.BlockSpec(memory_space=pltpu.HBM)
ANY = pl.BlockSpec(memory_space=pl.ANY)
VMEM = pl.BlockSpec(memory_space=pltpu.VMEM)
PARAMS = pltpu.CompilerParams(vmem_limit_bytes=32 * 1024 * 1024)


def shaped(*shape):
    return jax.ShapeDtypeStruct(shape, jnp.bfloat16)


def window(info, h, j):
    return STORED - info[h, j]


def vertical_block(info, h, v):
    return info[h, FREE + v]


def member(chip):
    return (chip >> 3) * 2 + (chip & 1)


def plane_row(chip):
    return (chip >> 1) & 3


END_ROWS = tuple(plane_row(end) for end in ENDS)


def wait_for(sem, count, like):
    def one(_, carry):
        pltpu.make_async_copy(like, like, sem).wait()
        return carry

    lax.fori_loop(0, count, one, 0)


def cached_block(core, h, block, mine, other, test, act):
    at = ((block >> 1) & 31, block & 1, slice(None), pl.ds(h * HD, HD))
    here = ((block >> 6) & 1) == core

    @pl.when(here & test)
    def _():
        act(mine[0].at[at], mine[1].at[at])

    @pl.when(jnp.logical_not(here) & test)
    def _():
        act(other[0].at[at], other[1].at[at])


def pack_first(info, keys, values, other_keys, other_values, out, sem, end_sem):
    chip, core = info[0, CHIP], info[0, CORE]
    ends = []
    for end, pair, caches in (
        (ENDS[0], 0, (keys, values)),
        (ENDS[1], 16, (other_keys, other_values)),
    ):
        copies = [
            pltpu.make_async_copy(
                cache.at[pl.ds(pair + (to >> 1) * 4, 4), to & 1, :, pl.ds(h * HD, HD)],
                out.at[to, :, 2 * h + k],
                end_sem,
            )
            for to in range(8)
            for h in range(KVS)
            for k, cache in enumerate(caches)
        ]
        ends.append((end, copies))

        @pl.when(chip == end)
        def _(copies=copies):
            for c in copies:
                c.start()

    base = jnp.where((chip == ENDS[0]) | (chip == ENDS[1]), KVS, 0)
    spans = []
    for h, j in PAIRS:
        start = window(info, h, j)
        first = jnp.clip(chip * PER_CHIP - start, 0, 32)
        last = jnp.clip((chip + 1) * PER_CHIP - start, 0, 32)
        spans.append((start, first, last))
    started = jnp.int32(0)
    for i, (h, _) in enumerate(PAIRS):
        start, first, last = spans[i]

        def one(block, count, i=i, h=h, start=start):
            lane = base
            for _, a, b in spans[:i]:
                lane = lane + jnp.where((block >= a) & (block < b), 1, 0)
            row, to = plane_row(block), member(block)

            def act(key_rows, value_rows):
                pltpu.make_async_copy(key_rows, out.at[to, row, lane * 2], sem).start()
                pltpu.make_async_copy(value_rows, out.at[to, row, lane * 2 + 1], sem).start()

            block = start + block
            cached_block(core, h, block, (keys, values), (other_keys, other_values), True, act)
            return count + 2

        started = lax.fori_loop(first, last, one, started)
    wait_for(sem, started, out.at[0, 0, 0])
    for end, copies in ends:

        @pl.when(chip == end)
        def _(copies=copies):
            for c in copies:
                c.wait()


def first_call(info, cached, lanes):
    return pl.pallas_call(
        pack_first,
        out_shape=shaped(8, 4, lanes * 2, BLOCK, HD),
        in_specs=[SMEM, HBM, HBM, ANY, ANY],
        out_specs=VMEM,
        scratch_shapes=[pltpu.SemaphoreType.DMA, pltpu.SemaphoreType.DMA],
        compiler_params=PARAMS,
        name="pack_first",
    )(info, *cached)


def sources_of(info, block):
    return [(window(info, h, j) + block) >> 7 for h, j in PAIRS]


def rank_of(i, keys, fixed):
    rank = jnp.where((keys[i] == fixed[0]) | (keys[i] == fixed[1]), KVS, 0)
    for before in keys[:i]:
        rank = rank + jnp.where(before == keys[i], 1, 0)
    return rank


def pack_second(info, got, out):
    chip = info[0, CHIP]
    row_here = plane_row(chip)
    for end in ENDS:

        @pl.when(row_here == plane_row(end))
        def _(end=end):
            for zh in range(4):
                out[zh, : 2 * KVS] = got[member(end), zh, : 2 * KVS]

    for zh in range(4):
        sources = sources_of(info, (chip & 25) + zh * 2)
        rows = [plane_row(source) for source in sources]
        for i in range(len(PAIRS)):

            @pl.when(rows[i] == row_here)
            def _(zh=zh, i=i, sources=sources, rows=rows):
                lane = rank_of(i, sources, ENDS)
                slot = rank_of(i, rows, END_ROWS)
                out[zh, pl.ds(slot * 2, 2)] = got[member(sources[i]), zh, pl.ds(lane * 2, 2)]


def second_call(info, got, slots):
    return pl.pallas_call(
        pack_second,
        out_shape=shaped(4, slots * 2, BLOCK, HD),
        in_specs=[SMEM, VMEM],
        out_specs=VMEM,
        compiler_params=PARAMS,
        name="pack_second",
    )(info, got)


def pack_queries(core, queries, new_keys, new_values, send):
    other = 1 - core
    for g in range(GROUP):
        at = TRADED + g * OWN
        send[at : at + OWN] = queries[:, (other * GROUP + g) * HD : (other * GROUP + g + 1) * HD]
    at = TRADED + GROUP * OWN
    send[at : at + OWN] = new_keys[:, other * HD : (other + 1) * HD]
    send[at + OWN : at + 2 * OWN] = new_values[:, other * HD : (other + 1) * HD]


def finish_slash(info, got, queries, new_keys, new_values, keep, send):
    rows = [plane_row(source) for source in sources_of(info, info[0, CHIP])]
    for h in range(KVS):
        for j in range(NS):
            if j < FREE:
                i = PAIRS.index((h, j))
                frm, slot = rows[i], rank_of(i, rows, END_ROWS) * 2
            else:
                frm, slot = END_ROWS[j - FREE], h * 2
            if h == 0:
                keep[j] = got[frm, pl.ds(slot, 2)]
            else:
                send[j * 2 * BLOCK : (j * 2 + 1) * BLOCK] = got[frm, slot]
                send[(j * 2 + 1) * BLOCK : (j + 1) * 2 * BLOCK] = got[frm, slot + 1]
    pack_queries(0, queries, new_keys, new_values, send)


def finish_vertical(info, got, queries, new_keys, new_values, keep, send):
    for v in range(NV):
        keep[v] = got[v, 2:]
        send[v * 2 * BLOCK : (v * 2 + 1) * BLOCK] = got[v, 0]
        send[(v * 2 + 1) * BLOCK : (v + 1) * 2 * BLOCK] = got[v, 1]
    pack_queries(1, queries, new_keys, new_values, send)


def finish_call(kernel, info, got, rows):
    return pl.pallas_call(
        kernel,
        out_shape=(shaped(NV, 2, BLOCK, HD), shaped(TRADED + (GROUP + 2) * OWN, HD)),
        in_specs=[SMEM] + [VMEM] * 4,
        out_specs=(VMEM, VMEM),
        compiler_params=PARAMS,
        name=kernel.__name__,
    )(info, got, *rows)


def pack_vertical(info, keys, values, other_keys, other_values, out, sem):
    chip, core = info[0, CHIP], info[0, CORE]
    started = jnp.int32(0)
    for h in range(KVS):
        for v in range(NV):
            block = vertical_block(info, h, v)
            mine = (block >> 7) == chip

            def act(key_rows, value_rows, h=h, v=v):
                pltpu.make_async_copy(key_rows, out.at[v, 2 * h], sem).start()
                pltpu.make_async_copy(value_rows, out.at[v, 2 * h + 1], sem).start()

            cached_block(core, h, block, (keys, values), (other_keys, other_values), mine, act)
            started = started + jnp.where(mine, 2, 0)
    wait_for(sem, started, out.at[0, 0])


def pack_vertical_call(info, cached):
    return pl.pallas_call(
        pack_vertical,
        out_shape=shaped(NV, 2 * KVS, BLOCK, HD),
        in_specs=[SMEM, HBM, HBM, ANY, ANY],
        out_specs=VMEM,
        scratch_shapes=[pltpu.SemaphoreType.DMA],
        compiler_params=PARAMS,
        name="pack_vertical",
    )(info, *cached)


def spread_rows(info, got, out):
    here = member(info[0, CHIP])
    for h in range(KVS):
        mine = got[member(vertical_block(info, h, here) >> 7), 2 * h : 2 * h + 2]
        for to in range(4):
            out[to, 2 * h : 2 * h + 2] = mine


def spread_members(info, got, out):
    here = member(info[0, CHIP])
    for h in range(KVS):
        mine = got[plane_row(vertical_block(info, h, here) >> 7), 2 * h : 2 * h + 2]
        for to in range(NV):
            out[to, 2 * h : 2 * h + 2] = mine


def spread_call(kernel, copies, info, got):
    return pl.pallas_call(
        kernel,
        out_shape=shaped(copies, 2 * KVS, BLOCK, HD),
        in_specs=[SMEM, VMEM],
        out_specs=VMEM,
        compiler_params=PARAMS,
        name=kernel.__name__,
    )(info, got)


COLS = (NV + NS + 2) * BLOCK
CHUNK = 256


def attend(info, queries, new_keys, new_values, keep, theirs, out, keys, values, rows):
    chip, core = info[0, CHIP], info[0, CORE]
    ours = core == 0
    verticals, slashes = 0, NV * BLOCK

    @pl.when(ours)
    def _():
        for j in range(NS):
            at = slashes + j * BLOCK
            keys[at : at + BLOCK] = keep[j, 0]
            values[at : at + BLOCK] = keep[j, 1]
        for v in range(NV):
            at = verticals + v * BLOCK
            keys[at : at + BLOCK] = theirs[v * 2 * BLOCK : (v * 2 + 1) * BLOCK]
            values[at : at + BLOCK] = theirs[(v * 2 + 1) * BLOCK : (v + 1) * 2 * BLOCK]

    @pl.when(jnp.logical_not(ours))
    def _():
        for j in range(NS):
            at = slashes + j * BLOCK
            keys[at : at + BLOCK] = theirs[j * 2 * BLOCK : (j * 2 + 1) * BLOCK]
            values[at : at + BLOCK] = theirs[(j * 2 + 1) * BLOCK : (j + 1) * 2 * BLOCK]
        for v in range(NV):
            at = verticals + v * BLOCK
            keys[at : at + BLOCK] = keep[v, 0]
            values[at : at + BLOCK] = keep[v, 1]

    column = lax.broadcasted_iota(jnp.int32, (1, COLS), 1)
    allowed = column < (NV + NS) * BLOCK
    for j in range(NS):
        start = window(info, core, j) if j < FREE else (0, STORED - 32)[j - FREE]
        block = start + chip
        at = slashes + j * BLOCK
        repeated = jnp.int32(0)
        for v in range(NV):
            repeated = repeated | jnp.where(vertical_block(info, core, v) == block, 1, 0)
        here = (column >= at) & (column < at + BLOCK)
        allowed = allowed & jnp.logical_not(here & (repeated == 1))
    mine = pl.multiple_of(core * OWN, OWN)
    rest = pl.multiple_of((1 - core) * OWN, OWN)
    for g in range(GROUP):
        cols = pl.ds(pl.multiple_of((core * GROUP + g) * HD, HD), HD)
        rows[pl.ds(mine + g * BLOCK, OWN)] = queries[:, cols]
        at = TRADED + g * OWN
        rows[pl.ds(rest + g * BLOCK, OWN)] = theirs[at : at + OWN]
    at = (NV + NS) * BLOCK
    cols = pl.ds(pl.multiple_of(core * HD, HD), HD)
    fresh = TRADED + GROUP * OWN
    keys[pl.ds(mine + at, OWN)] = new_keys[:, cols]
    values[pl.ds(mine + at, OWN)] = new_values[:, cols]
    keys[pl.ds(rest + at, OWN)] = theirs[fresh : fresh + OWN]
    values[pl.ds(rest + at, OWN)] = theirs[fresh + OWN : fresh + 2 * OWN]
    keys[at + BLOCK :] = jnp.zeros((BLOCK, HD), jnp.bfloat16)
    values[at + BLOCK :] = jnp.zeros((BLOCK, HD), jnp.bfloat16)
    row = lax.broadcasted_iota(jnp.int32, (CHUNK, COLS), 0) & (BLOCK - 1)
    col = lax.broadcasted_iota(jnp.int32, (CHUNK, COLS), 1)
    own = (col >= at) & (col - at <= row) & (col < at + BLOCK)
    kept = own | allowed
    scale = math.log2(math.e) / math.sqrt(HD)
    per = CHUNK // BLOCK
    for pair in range(GROUP // per):
        scores = lax.dot_general(
            rows[pair * CHUNK : (pair + 1) * CHUNK],
            keys[...],
            (((1,), (1,)), ((), ())),
            preferred_element_type=jnp.float32,
        )
        scores = jnp.where(kept, scores, NEGATIVE)
        peak = jnp.max(scores, axis=-1, keepdims=True)
        weights = jnp.exp2((scores - peak) * scale)
        total = jnp.sum(weights, axis=-1, keepdims=True)
        acc = jnp.dot(
            weights.astype(jnp.bfloat16), values[...], preferred_element_type=jnp.float32
        )
        result = (acc / total).astype(jnp.bfloat16)
        for i in range(per):
            cols = slice((pair * per + i) * HD, (pair * per + i + 1) * HD)
            for c in range(2):
                for y in range(4):
                    r = i * BLOCK + c * 32 + y * 8
                    out[y * 2 + c, :, cols] = result[r : r + 8]


def attend_call(info, rows, keep, theirs):
    return pl.pallas_call(
        attend,
        out_shape=shaped(8, 8, GROUP * HD),
        in_specs=[SMEM] + [VMEM] * 5,
        out_specs=VMEM,
        scratch_shapes=[
            pltpu.VMEM((COLS, HD), jnp.bfloat16),
            pltpu.VMEM((COLS, HD), jnp.bfloat16),
            pltpu.VMEM((GROUP * BLOCK, HD), jnp.bfloat16),
        ],
        compiler_params=PARAMS,
        name="attend",
    )(info, *rows, keep, theirs)


def choice_of(slash):
    blocks = jnp.arange(32, dtype=jnp.int32)
    chips = ((STORED + blocks[None, None, :] - slash[:, :, None]) >> 7).reshape(KVS * NS, 32)
    keys = jnp.stack([chips, plane_row(chips)])
    same = (keys[:, :, None, :] == keys[:, None, :, :]).astype(jnp.int32)
    most = jnp.max(jnp.sum(same, axis=2), axis=(1, 2))
    chosen = jnp.int32(0)
    for i, sizes in enumerate((LANES, SLOTS)):
        chosen = chosen * len(sizes) + sum((most[i] > n).astype(jnp.int32) for n in sizes[:-1])
    return chosen


def exchange(blocks, axes):
    return lax.all_to_all(blocks, axes, 0, 0, tiled=True)


def body(queries, cache_keys, cache_values, new_keys, new_values, vertical, slash):
    core = lax.axis_index("c").astype(jnp.int32)
    chip = (
        lax.axis_index("x") * 8 + lax.axis_index("zh") * 2 + lax.axis_index("zp")
    ).astype(jnp.int32)
    choice = choice_of(slash)
    here = jnp.broadcast_to(jnp.stack([chip, core, choice]), (2, 3))
    fixed = (slash == 32) | (slash == STORED)
    free = jnp.stack(
        [
            jnp.min(jnp.where(fixed, STORED, slash), axis=1),
            jnp.max(jnp.where(fixed, 32, slash), axis=1),
        ],
        axis=1,
    )
    info = jnp.concatenate([free, vertical, here], axis=1)
    rows = (queries, new_keys, new_values)
    swap = [(0, 1), (1, 0)]
    cached = (
        cache_keys,
        cache_values,
        lax.ppermute(cache_keys, "c", swap),
        lax.ppermute(cache_values, "c", swap),
    )
    cached = tuple(a.reshape(32, 2, BLOCK, KVS * HD) for a in cached)
    cached = tuple(pltpu.with_memory_space_constraint(a, pltpu.HBM) for a in cached[:2]) + cached[2:]

    def slashes(lanes, slots):
        got = exchange(first_call(info, cached, lanes), ("x", "zp"))
        got = exchange(second_call(info, got, slots), "zh")
        return finish_call(finish_slash, info, got, rows)

    def verticals():
        got = exchange(pack_vertical_call(info, cached), ("x", "zp"))
        got = exchange(spread_call(spread_rows, 4, info, got), "zh")
        got = exchange(spread_call(spread_members, NV, info, got), ("x", "zp"))
        return finish_call(finish_vertical, info, got, rows)

    ways = [functools.partial(slashes, n, m) for n in LANES for m in SLOTS]
    keep, send = lax.switch(jnp.where(core == 0, 1 + choice, 0), [verticals] + ways)
    theirs = lax.ppermute(send, "c", swap)
    out = attend_call(info, rows, keep, theirs)
    out = lax.all_to_all(out, ("y", "c"), 0, 0, tiled=True)
    return out.transpose(1, 0, 2).reshape(8, 8 * GROUP * HD)


def solution(mesh):
    parts = Mesh(mesh.devices.reshape(4, 4, 2, 2, 4), ("x", "zh", "zp", "c", "y"))
    ctx = ("x", "zh", "zp", "c")
    in_specs = (P(ctx, "y"),) * 5 + (P("y", None),) * 2
    out_specs = P(ctx + ("y",), None)
    return jax.shard_map(body, mesh=parts, in_specs=in_specs, out_specs=out_specs, check_vma=False)
```
